32 devices in a mesh: groups: 2 (over x), dp: 8 (over z, y), tensor: 2 (over core).
Axes of the slice: x: 2, y: 2, z: 4, core: 2. Of those that a mesh axis runs over, the one named last changes fastest.
Arguments:
- hidden_in: bfloat16 [256, 4096], P(('groups', 'dp')), parts along dimension 0, may hold values from -6 to 6
- grad_out: bfloat16 [256, 4096], P(('groups', 'dp')), parts along dimension 0, may hold values from -6 to 6
- norm_gain: float32 [4096], replicated, may hold values from 0.5 to 1.5
- gate_weight: bfloat16 [4096, 16384], P(None, ('dp', 'tensor')), may hold values from -0.09375 to 0.09375
- up_weight: bfloat16 [4096, 16384], P(None, ('dp', 'tensor')), may hold values from -0.09375 to 0.09375
- down_weight: bfloat16 [16384, 4096], P(('dp', 'tensor')), may hold values from -0.046875 to 0.046875
- tenant_basis: bfloat16 [16, 8, 4096], P(('groups', 'dp')), parts along dimension 0, may hold values from -0.09375 to 0.09375
- tenant_learned: bfloat16 [16, 8, 4096], P(('groups', 'dp')), parts along dimension 0, may hold values from -0.09375 to 0.09375
- tenant_bias: bfloat16 [16, 8], P(('groups', 'dp')), parts along dimension 0, may hold values from -4 to 4
- row_counts: int32 [16], P('groups'), parts along dimension 0, may hold values from 0 to 80, as said below
- segment_starts: int32 [16], P('groups'), parts along dimension 0, may hold values from 0 to 128, as said below
- owner_slot: int32 [16], P('groups'), parts along dimension 0, may hold values from 0 to 7, each once
Outputs:
- grad_hidden: bfloat16 [256, 4096], P(('groups', 'dp')), parts along dimension 0
- grad_basis: float32 [16, 8, 4096], P(('groups', 'dp')), parts along dimension 0
- grad_learned: float32 [16, 8, 4096], P(('groups', 'dp')), parts along dimension 0
- grad_bias: float32 [16, 8], P(('groups', 'dp')), parts along dimension 0
The draws below stay inside these ranges and needn't reach their ends.
There are 2 independent parts, one for each index of `groups`. The reference program is written for one: setup_inputs(seed, part) draws one part's arguments, and reference() takes and returns one part's arrays. A program takes and returns all parts, laid end to end along the dimension named above; an argument that names none is the same for every part. Nothing has to cross between parts.
Inputs may be any that keep to these rules, and one draw needn't show every extreme that they name: Tenant segments lie in tenant order end to end over all 128 rows; tenant t covers ceil(row_counts[t] / 16) blocks of 16 rows; 4 tenants have rows, the others none; one tenant covers exactly 5 blocks and holds 80 rows. segment_starts[t] is 16 times the blocks of all tenants before t; the last tenant has no rows.
All inputs are finite; a program needn't handle non-finite values.
Results may differ from the reference program's by a relative error of at most 0.0059.
Values may be sent and summed in bfloat16 or wider, within the bound.
No kernel may reach another device: no remote copies, remote signals or barrier semaphores. Data moves between devices by JAX's collectives and lax.ppermute only.
A program may use at most 128 MiB of HBM per device.

```python
import jax
import jax.numpy as jnp
from jax import lax

D = 4096
FF = 16384
RANK = 8
SEG = 16
TOKENS = 128
TENANTS = 8
BLOCKS = 8
ACTIVE = 4
MOST = 5


def segment_draw(key):
    extra = BLOCKS - MOST
    base_blocks = extra // (ACTIVE - 1)
    leftover = extra % (ACTIVE - 1)
    ranks = jnp.arange(ACTIVE, dtype=jnp.int32)
    pattern = jnp.where(ranks == 0, MOST, base_blocks + (ranks - 1 < leftover).astype(jnp.int32))
    shuffled = jax.random.permutation(jax.random.fold_in(key, 5), TENANTS - 1).astype(jnp.int32)
    order = jnp.argsort(shuffled, stable=True).astype(jnp.int32)
    order = jnp.concatenate([order, jnp.full((1,), TENANTS - 1, dtype=jnp.int32)])
    picked = jnp.minimum(order, ACTIVE - 1)
    blocks = jnp.where(order < ACTIVE, pattern[picked], 0).astype(jnp.int32)
    padding = jax.random.randint(jax.random.fold_in(key, 6), (TENANTS,), 0, SEG)
    padding = jnp.where(order == 0, 0, padding)
    counts = jnp.where(blocks > 0, blocks * SEG - padding, 0)
    starts = (jnp.cumsum(blocks) - blocks) * SEG
    return (counts.astype(jnp.int32), starts.astype(jnp.int32))


def draw_row_counts(key, part):
    counts, starts = segment_draw(key)
    return counts


def draw_segment_starts(key, part):
    counts, starts = segment_draw(key)
    return starts


def block_scale(key, dims, shards, least, largest):
    def one(dim, shards_of):
        draws = jax.random.uniform(jax.random.fold_in(jax.random.fold_in(key, 6), dim), (shards_of,), jnp.float32, least / len(shards), largest / len(shards))
        return jnp.repeat(jnp.exp(draws), dims[dim] // shards_of).reshape((-1,) + (1,) * (len(dims) - dim - 1))

    loudness = one(*shards[0])
    for cut in shards[1:]:
        loudness = loudness * one(*cut)
    return loudness


def normal_values(own_key, extent, width, limit, cuts=(), kind=jnp.bfloat16):
    values = width * jax.random.normal(own_key, extent, jnp.float32)
    if cuts:
        values = values * block_scale(own_key, extent, cuts, -0.22, 0.18)
    return jnp.clip(values, -limit, limit).astype(kind)


def setup_inputs(seed: int = 0, part: int = 0) -> dict:
    keys = jax.random.split(jax.random.key(seed), 13)
    part_splits = jax.random.split(jax.random.fold_in(keys[12], part), 13)
    hidden_in = normal_values(part_splits[0], (TOKENS, D), 1.0, 6.0, ((0, 8),))
    grad_out = normal_values(part_splits[1], (TOKENS, D), 1.0, 6.0, ((0, 8),))
    norm_gain = jnp.clip(1.0 + 0.1 * jax.random.normal(keys[2], (D,), jnp.float32), 0.5, 1.5)
    gate_weight = normal_values(keys[3], (D, FF), D ** -0.5, 0.09375, ((1, 16),))
    up_weight = normal_values(keys[4], (D, FF), D ** -0.5, 0.09375, ((1, 16),))
    down_weight = normal_values(keys[5], (FF, D), FF ** -0.5, 0.046875, ((0, 16),))
    tenant_basis = normal_values(part_splits[6], (TENANTS, RANK, D), D ** -0.5, 0.09375, ((0, 8),))
    tenant_learned = normal_values(part_splits[7], (TENANTS, RANK, D), D ** -0.5, 0.09375, ((0, 8),))
    tenant_bias = normal_values(part_splits[8], (TENANTS, RANK), 1.0, 4.0, ((0, 8),))
    row_counts = draw_row_counts(jax.random.fold_in(jax.random.fold_in(keys[12], part), 71), part)
    segment_starts = draw_segment_starts(jax.random.fold_in(jax.random.fold_in(keys[12], part), 71), part)
    owner_slot = jax.random.permutation(part_splits[11], TENANTS).astype(jnp.int32)
    return dict(hidden_in=hidden_in, grad_out=grad_out, norm_gain=norm_gain, gate_weight=gate_weight, up_weight=up_weight, down_weight=down_weight, tenant_basis=tenant_basis, tenant_learned=tenant_learned, tenant_bias=tenant_bias, row_counts=row_counts, segment_starts=segment_starts, owner_slot=owner_slot)


def block_plan(row_counts, segment_starts, owner_slot, first_block, block_total):
    tenant_total = segment_starts.shape[0]
    starts = (first_block + jnp.arange(block_total, dtype=jnp.int32)) * SEG
    below = (segment_starts[None, :] <= starts[:, None]).astype(jnp.int32)
    tenant_of = lax.optimization_barrier(jnp.sum(below, axis=1)) - 1
    match = tenant_of[:, None] == jnp.arange(tenant_total, dtype=jnp.int32)[None, :]
    block_start = lax.optimization_barrier(jnp.sum(jnp.where(match, segment_starts[None, :], 0), axis=1))
    block_count = lax.optimization_barrier(jnp.sum(jnp.where(match, row_counts[None, :], 0), axis=1))
    slots = lax.optimization_barrier(jnp.sum(jnp.where(match, owner_slot[None, :], 0), axis=1))
    position = starts[:, None] + jnp.arange(SEG, dtype=jnp.int32)[None, :] - block_start[:, None]
    live = (position < block_count[:, None]).astype(jnp.float32)
    return (slots, live)

def intervene(rows, basis_f, learned_f, bias_f, live):
    rows_f = rows.astype(jnp.float32)
    coeffs = jnp.einsum('bsd,brd->bsr', rows_f, learned_f - basis_f, precision=lax.Precision.HIGHEST)
    coeffs = (coeffs + bias_f[:, None, :]) * live[:, :, None]
    middle = rows_f + jnp.einsum('bsr,brd->bsd', coeffs, basis_f, precision=lax.Precision.HIGHEST)
    return (coeffs, middle.astype(jnp.bfloat16))

def hidden_terms(middle, upstream, norm_gain, gate_weight, up_weight, down_weight):
    middle_f = middle.astype(jnp.float32)
    inverse = lax.rsqrt(lax.optimization_barrier(jnp.mean(middle_f * middle_f, axis=-1, keepdims=True)) + 1e-05)
    normed = (middle_f * inverse * norm_gain).astype(jnp.bfloat16)
    gate = jnp.dot(normed, gate_weight, preferred_element_type=jnp.float32)
    upward = jnp.dot(normed, up_weight, preferred_element_type=jnp.float32)
    sigma = jax.nn.sigmoid(gate)
    back = jnp.dot(upstream, down_weight.T, preferred_element_type=jnp.float32)
    gate_grad = (back * upward * sigma * (1.0 + gate * (1.0 - sigma))).astype(jnp.bfloat16)
    up_grad = (back * gate * sigma).astype(jnp.bfloat16)
    first = jnp.dot(gate_grad, gate_weight.T, preferred_element_type=jnp.float32)
    return first + jnp.dot(up_grad, up_weight.T, preferred_element_type=jnp.float32)

def norm_back(middle, upstream, normal_grad, norm_gain):
    middle_f = middle.astype(jnp.float32)
    inverse = lax.rsqrt(lax.optimization_barrier(jnp.mean(middle_f * middle_f, axis=-1, keepdims=True)) + 1e-05)
    scaled = normal_grad * norm_gain
    inner = lax.optimization_barrier(jnp.mean(scaled * middle_f, axis=-1, keepdims=True))
    return upstream.astype(jnp.float32) + inverse * (scaled - middle_f * inverse * inverse * inner)

def intervene_back(rows, total, coeffs, basis_f, learned_f, live):
    rows_f = rows.astype(jnp.float32)
    pulled = jnp.einsum('bsd,brd->bsr', total, basis_f, precision=lax.Precision.HIGHEST) * live[:, :, None]
    grad_rows = total + jnp.einsum('bsr,brd->bsd', pulled, learned_f - basis_f, precision=lax.Precision.HIGHEST)
    grad_learn = jnp.einsum('bsr,bsd->brd', pulled, rows_f, precision=lax.Precision.HIGHEST)
    grad_base = jnp.einsum('bsr,bsd->brd', coeffs, total, precision=lax.Precision.HIGHEST) - grad_learn
    return (grad_rows.astype(jnp.bfloat16), grad_base, grad_learn, lax.optimization_barrier(jnp.sum(pulled, axis=1)))

def reference(hidden_in, grad_out, norm_gain, gate_weight, up_weight, down_weight, tenant_basis, tenant_learned, tenant_bias, row_counts, segment_starts, owner_slot):
    slots, live = block_plan(row_counts, segment_starts, owner_slot, 0, BLOCKS)
    tenant_hot = (slots[:, None] == jnp.arange(TENANTS, dtype=jnp.int32)[None, :]).astype(jnp.float32)
    basis_f = jnp.einsum('bs,srd->brd', tenant_hot, tenant_basis.astype(jnp.float32), precision=lax.Precision.HIGHEST)
    learned_f = jnp.einsum('bs,srd->brd', tenant_hot, tenant_learned.astype(jnp.float32), precision=lax.Precision.HIGHEST)
    bias_f = jnp.dot(tenant_hot, tenant_bias.astype(jnp.float32), precision=lax.Precision.HIGHEST)
    rows = hidden_in.reshape(BLOCKS, SEG, D)
    coeffs, middle = intervene(rows, basis_f, learned_f, bias_f, live)
    middle_rows = middle.reshape(TOKENS, D)
    normal_grad = hidden_terms(middle_rows, grad_out, norm_gain, gate_weight, up_weight, down_weight)
    total = norm_back(middle_rows, grad_out, normal_grad, norm_gain).reshape(BLOCKS, SEG, D)
    grad_rows, grad_base, grad_learn, grad_offset = intervene_back(rows, total, coeffs, basis_f, learned_f, live)
    out_basis = jnp.einsum('bs,brd->srd', tenant_hot, grad_base, precision=lax.Precision.HIGHEST)
    out_learned = jnp.einsum('bs,brd->srd', tenant_hot, grad_learn, precision=lax.Precision.HIGHEST)
    out_bias = jnp.dot(tenant_hot.T, grad_offset, precision=lax.Precision.HIGHEST)
    return (grad_rows.reshape(TOKENS, D), out_basis, out_learned, out_bias)
```

```python
import functools

import jax
import jax.numpy as jnp
from jax import lax
from jax.experimental import pallas as pl
from jax.experimental.pallas import tpu as pltpu
from jax.sharding import PartitionSpec as P

SEG = 16
RANK = 8
PAD = 128
EPS = 1e-05
BF = jnp.bfloat16
F32 = jnp.float32


def dot_nn(a, b):
    return jnp.dot(a, b, preferred_element_type=F32)


def dot_nt(a, b):
    return lax.dot_general(a, b, (((1,), (1,)), ((), ())), preferred_element_type=F32)


def split(x):
    high = x.astype(BF)
    low = (x - high.astype(F32)).astype(BF)
    return high, low


def ring_order(n):
    if n == 8:
        return [0, 2, 4, 6, 7, 5, 3, 1]
    return list(range(n))


def block_kernel(
    tile,
    step,
    mask_ref,
    rows_ref,
    tables_ref,
    upstream_ref,
    gain_ref,
    gate_hbm,
    up_hbm,
    down_hbm,
    own_ref,
    own_slot_ref,
    total_ref,
    slot_ref,
    gate_ref,
    up_ref,
    down_ref,
    middle_ref,
    normed_ref,
    scaled_ref,
    gate_grad_ref,
    up_grad_ref,
    sems,
):
    row_total, width = middle_ref.shape
    hidden = gate_ref.shape[1]
    tiles = hidden // tile
    chunks = width // step
    columns = tables_ref.shape[0]

    def weight_copies(j):
        cols = pl.ds(j * tile, tile)
        return (
            pltpu.make_async_copy(gate_hbm.at[:, cols], gate_ref.at[:, cols], sems.at[0, j]),
            pltpu.make_async_copy(up_hbm.at[:, cols], up_ref.at[:, cols], sems.at[1, j]),
            pltpu.make_async_copy(down_hbm.at[cols, :], down_ref.at[cols, :], sems.at[2, j]),
        )

    for j in range(tiles):
        for copy in weight_copies(j):
            copy.start()

    mask = mask_ref[...]
    lane = lax.broadcasted_iota(jnp.int32, (row_total, columns), 1)
    products = dot_nt(rows_ref[...], tables_ref[...])
    coeffs = mask * (pltpu.roll(products, columns - RANK, 1) - products)
    coeff_high, coeff_low = split(coeffs)
    pulled_up = dot_nt(upstream_ref[...], tables_ref[:, :width])
    first_slot = jnp.where(lane < RANK, 0.5, 0.0)

    def middle_step(c, squares):
        cols = pl.ds(pl.multiple_of(c * step, step), step)
        table = tables_ref[:, cols]
        value = rows_ref[:, cols].astype(F32) + (
            dot_nn(coeff_high, table) + dot_nn(coeff_low, table)
        )
        value = value.astype(BF)
        middle_ref[:, cols] = value
        value = value.astype(F32)
        return squares + jnp.sum(value * value, axis=1, keepdims=True)

    squares = lax.fori_loop(0, chunks, middle_step, jnp.zeros((row_total, 1), F32))
    inverse = lax.rsqrt(squares / width + EPS)

    def normed_step(c, carry):
        cols = pl.ds(pl.multiple_of(c * step, step), step)
        value = middle_ref[:, cols].astype(F32) * inverse * gain_ref[:, cols]
        normed_ref[:, cols] = value.astype(BF)
        return carry

    lax.fori_loop(0, chunks, normed_step, 0)

    for j in range(tiles):
        for copy in weight_copies(j):
            copy.wait()
        cols = pl.ds(j * tile, tile)
        gate = dot_nn(normed_ref[...], gate_ref[:, cols])
        upward = dot_nn(normed_ref[...], up_ref[:, cols])
        back = dot_nt(upstream_ref[...], down_ref[cols, :])
        sigma = jax.nn.sigmoid(gate)
        gate_grad_ref[:, cols] = (back * upward * sigma * (1.0 + gate * (1.0 - sigma))).astype(BF)
        up_grad_ref[:, cols] = (back * gate * sigma).astype(BF)

    def scaled_step(c, inner):
        cols = pl.ds(pl.multiple_of(c * step, step), step)
        value = dot_nt(gate_grad_ref[...], gate_ref[cols, :])
        value = value + dot_nt(up_grad_ref[...], up_ref[cols, :])
        value = value * gain_ref[:, cols]
        scaled_ref[:, cols] = value
        return inner + jnp.sum(value * middle_ref[:, cols].astype(F32), axis=1, keepdims=True)

    inner = lax.fori_loop(0, chunks, scaled_step, jnp.zeros((row_total, 1), F32))
    shrink = inverse * inverse * (inner / width)

    def total_step(c, pulled):
        cols = pl.ds(pl.multiple_of(c * step, step), step)
        value = inverse * (scaled_ref[:, cols] - middle_ref[:, cols].astype(F32) * shrink)
        scaled_ref[:, cols] = value
        high, low = split(value)
        total_ref[:, cols] = high
        own_ref[:, cols] = value[:SEG] + 0.5 * upstream_ref[:SEG, cols].astype(F32)
        table = tables_ref[:, cols]
        return pulled + (dot_nt(high, table) + dot_nt(low, table))

    pulled = lax.fori_loop(0, chunks, total_step, jnp.zeros((row_total, columns), F32))
    pulled = mask * (pulled + first_slot * pulled_up)
    pulled = pltpu.roll(pulled, RANK, 1) - pulled
    coeff_t = coeffs.T
    first_t = (coeffs * first_slot).T
    pulled_t = pulled.T
    coeff_high, coeff_low = split(coeff_t)
    first_high, first_low = split(first_t[:SEG])
    pulled_high, pulled_low = split(pulled_t)

    def slot_step(c, carry):
        cols = pl.ds(pl.multiple_of(c * step, step), step)
        high, low = split(scaled_ref[:, cols])
        rows = rows_ref[:, cols]
        value = dot_nn(coeff_high, high) + dot_nn(coeff_high, low) + dot_nn(coeff_low, high)
        value = value + dot_nn(pulled_high, rows) + dot_nn(pulled_low, rows)
        slot_ref[:, cols] = value.astype(BF)
        upstream = upstream_ref[:, cols]
        own_slot_ref[:, cols] = value[:SEG] + (
            dot_nn(first_high, upstream) + dot_nn(first_low, upstream)
        )
        return carry

    lax.fori_loop(0, chunks, slot_step, 0)
    extra = rows_ref[:, width:]
    value = dot_nn(pulled_high, extra) + dot_nn(pulled_low, extra)
    slot_ref[:, width:] = value.astype(BF)
    own_slot_ref[:, width:] = value[:SEG]


def block(mask, rows, tables, upstream, gain, gate_weight, up_weight, down_weight):
    row_total, width = upstream.shape
    wide = rows.shape[1]
    hidden = gate_weight.shape[1]
    tile = min(256, hidden)
    tiles = hidden // tile
    vmem = pl.BlockSpec(memory_space=pltpu.VMEM)
    hbm = pl.BlockSpec(memory_space=pl.ANY)
    return pl.pallas_call(
        functools.partial(block_kernel, tile, 512),
        out_shape=(
            jax.ShapeDtypeStruct((SEG, width), F32),
            jax.ShapeDtypeStruct((SEG, wide), F32),
            jax.ShapeDtypeStruct((row_total, width), BF),
            jax.ShapeDtypeStruct((row_total, wide), BF),
        ),
        in_specs=[vmem, vmem, vmem, vmem, vmem, hbm, hbm, hbm],
        out_specs=(vmem, vmem, vmem, vmem),
        scratch_shapes=[
            pltpu.VMEM((width, hidden), BF),
            pltpu.VMEM((width, hidden), BF),
            pltpu.VMEM((hidden, width), BF),
            pltpu.VMEM((row_total, width), BF),
            pltpu.VMEM((row_total, width), BF),
            pltpu.VMEM((row_total, width), F32),
            pltpu.VMEM((row_total, hidden), BF),
            pltpu.VMEM((row_total, hidden), BF),
            pltpu.SemaphoreType.DMA((3, tiles)),
        ],
        compiler_params=pltpu.CompilerParams(vmem_limit_bytes=58 * 1024 * 1024),
        cost_estimate=pl.CostEstimate(
            flops=10 * row_total * width * hidden,
            bytes_accessed=6 * width * hidden,
            transcendentals=row_total * hidden,
        ),
    )(mask, rows, tables, upstream, gain, gate_weight, up_weight, down_weight)


def plan(row_counts, segment_starts, owner_slot, blocks, own_slots):
    starts = blocks * SEG
    tenant_total = segment_starts.shape[0]
    tenant_of = jnp.sum((segment_starts[None, :] <= starts[:, None]).astype(jnp.int32), axis=1) - 1
    match = tenant_of[:, None] == jnp.arange(tenant_total, dtype=jnp.int32)[None, :]
    block_start = jnp.sum(jnp.where(match, segment_starts[None, :], 0), axis=1)
    block_count = jnp.sum(jnp.where(match, row_counts[None, :], 0), axis=1)
    slots = jnp.sum(jnp.where(match, owner_slot[None, :], 0), axis=1)
    position = starts[:, None] + jnp.arange(SEG, dtype=jnp.int32)[None, :] - block_start[:, None]
    live = (position < block_count[:, None]).astype(F32)
    pick = slots[:, None] == own_slots[None, :]
    mask = live[:, :, None] * pick[:, None, :].astype(F32)
    return live, pick, mask.reshape(-1, own_slots.shape[0])


def make_device_function(n):
    order = ring_order(n)
    place = {d: k for k, d in enumerate(order)}
    half = n // 2 - 1
    pairs = []
    for d in range(n):
        pairs.append((d * 2, order[(place[d] + 1) % n] * 2))
        pairs.append((d * 2 + 1, order[(place[d] - 1) % n] * 2 + 1))

    def hop(x):
        return lax.ppermute(x, ("dp", "tensor"), pairs)

    def swap(x):
        return lax.ppermute(x, "tensor", [(0, 1), (1, 0)])

    def on_device(
        hidden_in,
        grad_out,
        norm_gain,
        gate_weight,
        up_weight,
        down_weight,
        tenant_basis,
        tenant_learned,
        tenant_bias,
        row_counts,
        segment_starts,
        owner_slot,
    ):
        width = hidden_in.shape[1]
        ones = jnp.zeros((SEG, PAD), BF).at[:, 0].set(1)
        bias = jnp.pad(
            tenant_bias.reshape(RANK, 1), ((RANK, 0), (0, PAD - 1))
        )
        packed = jnp.concatenate(
            [
                jnp.concatenate([hidden_in, tenant_basis[0], tenant_learned[0]], axis=0),
                jnp.concatenate([ones, bias], axis=0),
            ],
            axis=1,
        )
        first, second = packed, grad_out
        ahead, behind = [], []
        for _ in range(half):
            first, second = hop(first), hop(second)
            ahead.append((first, second))
            behind.append((swap(first), swap(second)))
        pieces = [(packed, grad_out)] + ahead + behind + [(hop(first), hop(second))]
        rows = jnp.concatenate([a[:SEG] for a, _ in pieces], axis=0)
        tables = jnp.concatenate([a[SEG:] for a, _ in pieces], axis=0)
        upstream = jnp.concatenate([b for _, b in pieces], axis=0)

        core = lax.axis_index("tensor")
        me = jnp.array([place[d] for d in range(n)], jnp.int32)[lax.axis_index("dp")]
        away = jnp.array(
            [0] + [-t for t in range(1, half + 1)] + [t for t in range(1, half + 1)] + [n // 2],
            jnp.int32,
        )
        away = jnp.where(core == 0, away, -away)
        index = jnp.array(order, jnp.int32)[(me + away + n) % n]
        live, pick, mask = plan(row_counts, segment_starts, owner_slot, index, index)
        mask = jnp.repeat(mask, 2 * RANK, axis=1)
        column = jnp.arange(mask.shape[1], dtype=jnp.int32)
        mask = jnp.where(column[None, :] % (2 * RANK) < RANK, mask, 0.0)

        own, own_slot, total, slot = block(
            mask,
            rows,
            tables,
            upstream,
            norm_gain.reshape(1, width),
            gate_weight,
            up_weight,
            down_weight,
        )

        sent = slice(SEG, SEG * (1 + half))
        kept = SEG * (1 + half)
        far = SEG * (1 + 2 * half)
        results = []
        parts = []
        for value in (slot, total):
            parts.append((value, hop(value[far:]), swap(value[sent])))
        state = [p[1] for p in parts]
        for t in range(half - 1, -1, -1):
            for k, (value, _, other) in enumerate(parts):
                mine = value[kept + t * SEG : kept + (t + 1) * SEG].astype(F32)
                partner = other[t * SEG : (t + 1) * SEG].astype(F32)
                state[k] = hop((state[k].astype(F32) + (mine + partner)).astype(BF))
        for local, value in ((own_slot, state[0]), (own, state[1])):
            value = local + value.astype(F32)
            results.append(value + swap(value))
        slots, total = results

        which = jnp.sum(jnp.where(pick[0], jnp.arange(n, dtype=jnp.int32), 0))
        table = lax.dynamic_slice_in_dim(tables, which * SEG, SEG, 0)[:, :width].astype(F32)
        basis, learned = table[:RANK], table[RANK:]
        pulled = (
            lax.dot_general(
                total, basis, (((1,), (1,)), ((), ())), precision=lax.Precision.HIGHEST
            )
            * live[0][:, None]
        )
        grad_rows = total + jnp.dot(pulled, learned - basis, precision=lax.Precision.HIGHEST)
        return (
            grad_rows.astype(BF),
            slots[None, :RANK, :width],
            slots[None, RANK:, :width],
            slots[None, RANK:, width],
        )

    return on_device


def solution(mesh):
    return jax.shard_map(
        make_device_function(mesh.shape["dp"]),
        mesh=mesh,
        in_specs=(
            P(("groups", "dp"), None),
            P(("groups", "dp"), None),
            P(),
            P(None, ("dp", "tensor")),
            P(None, ("dp", "tensor")),
            P(("dp", "tensor"), None),
            P(("groups", "dp"), None, None),
            P(("groups", "dp"), None, None),
            P(("groups", "dp"), None),
            P("groups"),
            P("groups"),
            P("groups"),
        ),
        out_specs=(
            P(("groups", "dp"), None),
            P(("groups", "dp"), None, None),
            P(("groups", "dp"), None, None),
            P(("groups", "dp"), None),
        ),
        check_vma=False,
    )
```

```python
import functools

import jax
import jax.numpy as jnp
from jax import lax
from jax.experimental import pallas as pl
from jax.experimental.pallas import tpu as pltpu
from jax.sharding import PartitionSpec as P

SEG = 16
RANK = 8
PAD = 128
EPS = 1e-05
BF = jnp.bfloat16
F32 = jnp.float32


def dot_nn(a, b):
    return jnp.dot(a, b, preferred_element_type=F32)


def dot_nt(a, b):
    return lax.dot_general(a, b, (((1,), (1,)), ((), ())), preferred_element_type=F32)


def split(x):
    high = x.astype(BF)
    low = (x - high.astype(F32)).astype(BF)
    return high, low


def ring_order(n):
    if n == 8:
        return [0, 2, 4, 6, 7, 5, 3, 1]
    return list(range(n))


def place_of(n, d):
    if n == 8:
        return jnp.where(d % 2 == 0, d // 2, n - 1 - d // 2)
    return d


def device_at(n, p):
    if n == 8:
        return jnp.where(p < n // 2, 2 * p, 2 * (n - 1 - p) + 1)
    return p


def piece_devices(n, where_ref):
    half = n // 2 - 1
    steps = [0] + [-t for t in range(1, half + 1)] + [t for t in range(1, half + 1)] + [n // 2]
    me = place_of(n, where_ref[0])
    sign = 1 - 2 * where_ref[1]
    return [device_at(n, lax.rem(me + sign * step + n, n)) for step in steps]


def block_tenant(device, counts_ref, starts_ref, slots_ref):
    first = device * SEG
    begin, count, slot = starts_ref[0], counts_ref[0], slots_ref[0]
    for t in range(1, starts_ref.shape[0]):
        reached = starts_ref[t] <= first
        begin = jnp.where(reached, starts_ref[t], begin)
        count = jnp.where(reached, counts_ref[t], count)
        slot = jnp.where(reached, slots_ref[t], slot)
    return slot, count - (first - begin)


def tenant_mask(n, where_ref, counts_ref, starts_ref, slots_ref):
    shape = (n * SEG, n * SEG)
    row = lax.broadcasted_iota(jnp.int32, shape, 0)
    column = lax.broadcasted_iota(jnp.int32, shape, 1)
    devices = piece_devices(n, where_ref)
    row_slot = jnp.zeros(shape, jnp.int32)
    row_limit = jnp.zeros(shape, jnp.int32)
    column_slot = jnp.zeros(shape, jnp.int32)
    for k, device in enumerate(devices):
        slot, limit = block_tenant(device, counts_ref, starts_ref, slots_ref)
        here = row // SEG == k
        row_slot = jnp.where(here, slot, row_slot)
        row_limit = jnp.where(here, limit, row_limit)
        column_slot = jnp.where(column // SEG == k, device, column_slot)
    keep = (row_slot == column_slot) & (row % SEG < row_limit) & (column % SEG < RANK)
    return jnp.where(keep, 1.0, 0.0)


def columns_at(c, step):
    return pl.ds(pl.multiple_of(c * step, step), step)


def pack_kernel(
    hidden_hbm, basis_hbm, learned_hbm, bias_hbm, packed_ref, basis_ref, learned_ref, bias_ref, sems
):
    width = hidden_hbm.shape[1]
    copies = (
        pltpu.make_async_copy(hidden_hbm, packed_ref.at[:SEG, :width], sems.at[0]),
        pltpu.make_async_copy(basis_hbm, basis_ref, sems.at[1]),
        pltpu.make_async_copy(learned_hbm, learned_ref, sems.at[2]),
        pltpu.make_async_copy(bias_hbm, bias_ref, sems.at[3]),
    )
    for copy in copies:
        copy.start()
    for copy in copies:
        copy.wait()
    packed_ref[SEG:, :width] = jnp.concatenate(
        [basis_ref[0].astype(F32), learned_ref[0].astype(F32)], axis=0
    ).astype(BF)
    shape = (SEG, PAD)
    row = lax.broadcasted_iota(jnp.int32, shape, 0)
    lane = lax.broadcasted_iota(jnp.int32, shape, 1)
    packed_ref[:SEG, width:] = jnp.where(lane == 0, 1.0, 0.0).astype(BF)
    bias = jnp.zeros(shape, F32)
    wide = bias_ref[...].astype(F32)
    for r in range(RANK):
        bias = jnp.where((row == RANK + r) & (lane == 0), wide[:, r : r + 1], bias)
    packed_ref[SEG:, width:] = bias.astype(BF)


def mark_kernel(after, out_ref):
    del after
    out_ref[...] = jnp.zeros_like(out_ref)


def back_kernel(n, *refs):
    pieces, (down_ref, upstream_ref, back_ref) = refs[:n], refs[-3:]
    for k, piece in enumerate(pieces):
        upstream_ref[k * SEG : (k + 1) * SEG, :] = piece[...]
    back_ref[...] = dot_nt(upstream_ref[...], down_ref[...])


def hidden_kernel(n, step, *refs):
    where_ref, counts_ref, starts_ref, slots_ref = refs[:4]
    pieces = refs[4 : 4 + n]
    (
        gain_ref,
        back_ref,
        gate_ref,
        up_ref,
        own_ref,
        sent_ref,
        scaled_ref,
        rows_ref,
        tables_ref,
        middle_ref,
        coeffs_ref,
        stats_ref,
        normed_ref,
        gate_grad_ref,
        up_grad_ref,
    ) = refs[4 + n :]
    row_total, width = middle_ref.shape
    chunks = width // step
    for k, piece in enumerate(pieces):
        rows_ref[k * SEG : (k + 1) * SEG, :] = piece[:SEG, :]
        tables_ref[k * SEG : (k + 1) * SEG, :] = piece[SEG:, :]

    columns = tables_ref.shape[0]
    products = dot_nt(rows_ref[...], tables_ref[...])
    mask = tenant_mask(n, where_ref, counts_ref, starts_ref, slots_ref)
    coeffs = mask * (pltpu.roll(products, columns - RANK, 1) - products)
    coeffs_ref[...] = coeffs
    coeff_high, coeff_low = split(coeffs)

    def middle_step(c, squares):
        cols = columns_at(c, step)
        table = tables_ref[:, cols]
        value = rows_ref[:, cols].astype(F32) + (
            dot_nn(coeff_high, table) + dot_nn(coeff_low, table)
        )
        value = value.astype(BF)
        middle_ref[:, cols] = value
        value = value.astype(F32)
        return squares + jnp.sum(value * value, axis=1, keepdims=True)

    squares = lax.fori_loop(0, chunks, middle_step, jnp.zeros((row_total, 1), F32))
    inverse = lax.rsqrt(squares / width + EPS)

    def normed_step(c, carry):
        cols = columns_at(c, step)
        value = middle_ref[:, cols].astype(F32) * inverse * gain_ref[:, cols]
        normed_ref[:, cols] = value.astype(BF)
        return carry

    lax.fori_loop(0, chunks, normed_step, 0)

    hidden = gate_ref.shape[1]
    tile = min(256, hidden)
    for j in range(hidden // tile):
        cols = slice(j * tile, (j + 1) * tile)
        gate = dot_nn(normed_ref[...], gate_ref[:, cols])
        upward = dot_nn(normed_ref[...], up_ref[:, cols])
        back = back_ref[:, cols]
        sigma = jax.nn.sigmoid(gate)
        gate_grad_ref[:, cols] = (back * upward * sigma * (1.0 + gate * (1.0 - sigma))).astype(BF)
        up_grad_ref[:, cols] = (back * gate * sigma).astype(BF)

    def scaled_step(c, inner):
        cols = columns_at(c, step)
        value = dot_nt(gate_grad_ref[...], gate_ref[cols, :])
        value = value + dot_nt(up_grad_ref[...], up_ref[cols, :])
        value = value * gain_ref[:, cols]
        scaled_ref[:, cols] = value
        own_ref[:, cols] = value[:SEG]
        sent_ref[:, cols] = value[SEG:].astype(BF)
        return inner + jnp.sum(value * middle_ref[:, cols].astype(F32), axis=1, keepdims=True)

    inner = lax.fori_loop(0, chunks, scaled_step, jnp.zeros((row_total, 1), F32))
    lane = lax.broadcasted_iota(jnp.int32, stats_ref.shape, 1)
    stats_ref[...] = jnp.where(lane == 0, inverse, inverse * inverse * (inner / width))


def slot_kernel(
    n,
    step,
    where_ref,
    counts_ref,
    starts_ref,
    slots_ref,
    scaled_ref,
    rows_ref,
    tables_ref,
    upstream_ref,
    middle_ref,
    coeffs_ref,
    stats_ref,
    own_ref,
    sent_ref,
    total_ref,
):
    row_total, width = middle_ref.shape
    columns = tables_ref.shape[0]
    chunks = width // step
    inverse, shrink = stats_ref[:, 0:1], stats_ref[:, 1:2]

    def total_step(c, carry):
        pulled, pulled_up = carry
        cols = columns_at(c, step)
        value = inverse * (scaled_ref[:, cols] - middle_ref[:, cols].astype(F32) * shrink)
        high, low = split(value)
        total_ref[0, :, cols] = high
        total_ref[1, :, cols] = low
        table = tables_ref[:, cols]
        pulled = pulled + (dot_nt(high, table) + dot_nt(low, table))
        return pulled, pulled_up + dot_nt(upstream_ref[:, cols], table)

    zero = jnp.zeros((row_total, columns), F32)
    pulled, pulled_up = lax.fori_loop(0, chunks, total_step, (zero, zero))
    mask = tenant_mask(n, where_ref, counts_ref, starts_ref, slots_ref)
    lane = lax.broadcasted_iota(jnp.int32, (row_total, columns), 1)
    first_slot = jnp.where(lane < RANK, 0.5, 0.0)
    pulled = mask * (pulled + first_slot * pulled_up)
    pulled = pltpu.roll(pulled, RANK, 1) - pulled
    coeffs = coeffs_ref[...]
    coeff_high, coeff_low = split(coeffs.T)
    first_high, first_low = split((coeffs * first_slot).T[:SEG])
    pulled_high, pulled_low = split(pulled.T)

    def slot_step(c, carry):
        cols = columns_at(c, step)
        high, low = total_ref[0, :, cols], total_ref[1, :, cols]
        rows = rows_ref[:, cols]
        value = dot_nn(coeff_high, high) + dot_nn(coeff_high, low) + dot_nn(coeff_low, high)
        value = value + dot_nn(pulled_high, rows) + dot_nn(pulled_low, rows)
        sent_ref[:, cols] = value[SEG:].astype(BF)
        upstream = upstream_ref[:, cols]
        own_ref[:, cols] = value[:SEG] + (
            dot_nn(first_high, upstream) + dot_nn(first_low, upstream)
        )
        return carry

    lax.fori_loop(0, chunks, slot_step, 0)
    extra = rows_ref[:, width:]
    value = dot_nn(pulled_high, extra) + dot_nn(pulled_low, extra)
    sent_ref[:, width:] = value[SEG:].astype(BF)
    own_ref[:, width:] = value[:SEG]


def rows_kernel(
    n,
    where_ref,
    counts_ref,
    starts_ref,
    slots_ref,
    mine_ref,
    other_ref,
    upstream_ref,
    middle_ref,
    stats_ref,
    tables_ref,
    out_ref,
):
    width = out_ref.shape[1]
    devices = piece_devices(n, where_ref)
    slot, limit = block_tenant(devices[0], counts_ref, starts_ref, slots_ref)
    which = 0
    for k, device in enumerate(devices):
        which = jnp.where(device == slot, k, which)
    table = tables_ref[pl.ds(pl.multiple_of(which * SEG, SEG), SEG), :width]
    middle = middle_ref[:SEG, :].astype(F32)
    inverse = stats_ref[:SEG, 0:1]
    scaled = mine_ref[...] + other_ref[...]
    inner = jnp.sum(scaled * middle, axis=1, keepdims=True) / width
    total = upstream_ref[...].astype(F32) + inverse * (
        scaled - middle * (inverse * inverse * inner)
    )
    high, low = split(total)
    pulled = dot_nt(high, table) + dot_nt(low, table)
    row = lax.broadcasted_iota(jnp.int32, (SEG, RANK), 0)
    pulled = jnp.where(row < limit, pulled[:, :RANK], 0.0)
    pulled = jnp.concatenate([-pulled, pulled], axis=1)
    high, low = split(pulled)
    out_ref[...] = (total + dot_nn(high, table) + dot_nn(low, table)).astype(BF)


LOAD_FLOPS = 4 * 10**9
LONG_FLOPS = 40 * 10**9
SMEM_SPEC = pl.BlockSpec(memory_space=pltpu.SMEM)
VMEM_SPEC = pl.BlockSpec(memory_space=pltpu.VMEM)


def call(kernel, outs, scalars, arrays, scratch=(), flops=0, moved=0, limit=4, spec=None):
    return pl.pallas_call(
        kernel,
        out_shape=tuple(jax.ShapeDtypeStruct(s, d) for s, d in outs),
        in_specs=[SMEM_SPEC] * len(scalars) + [spec or VMEM_SPEC] * len(arrays),
        out_specs=tuple(VMEM_SPEC for _ in outs),
        scratch_shapes=list(scratch),
        compiler_params=pltpu.CompilerParams(vmem_limit_bytes=limit * 1024 * 1024),
        cost_estimate=pl.CostEstimate(flops=flops, bytes_accessed=moved, transcendentals=0),
    )(*scalars, *arrays)


def resident(x):
    return pltpu.with_memory_space_constraint(x, pltpu.VMEM)


def remote(x):
    return pltpu.with_memory_space_constraint(x, pltpu.HBM)


def mark(after):
    (out,) = call(
        mark_kernel, [((8, 128), F32)], (), (after,), flops=LOAD_FLOPS, spec=pl.BlockSpec(memory_space=pl.ANY)
    )
    return out


def make_device_function(n):
    order = ring_order(n)
    place = {d: k for k, d in enumerate(order)}
    half = n // 2 - 1
    pairs = []
    for d in range(n):
        pairs.append((d * 2, order[(place[d] + 1) % n] * 2))
        pairs.append((d * 2 + 1, order[(place[d] - 1) % n] * 2 + 1))

    def hop(x):
        return lax.ppermute(x, ("dp", "tensor"), pairs)

    def swap(x):
        return lax.ppermute(x, "tensor", [(0, 1), (1, 0)])

    def gather(x):
        ahead, behind = [], []
        state = x
        for _ in range(half):
            state = hop(state)
            ahead.append(state)
            behind.append(swap(state))
        return [x] + ahead + behind + [hop(state)]

    def reduce(own, sent):
        other = swap(sent[: half * SEG])
        state = hop(sent[2 * half * SEG :])
        for t in range(half - 1, -1, -1):
            mine = sent[(half + t) * SEG : (half + t + 1) * SEG].astype(F32)
            partner = other[t * SEG : (t + 1) * SEG].astype(F32)
            state = hop((state.astype(F32) + (mine + partner)).astype(BF))
        return own + state.astype(F32)

    def on_device(
        hidden_in,
        grad_out,
        norm_gain,
        gate_weight,
        up_weight,
        down_weight,
        tenant_basis,
        tenant_learned,
        tenant_bias,
        row_counts,
        segment_starts,
        owner_slot,
    ):
        width = hidden_in.shape[1]
        hidden = gate_weight.shape[1]
        wide = width + PAD
        rows_total = n * SEG
        work = 2 * rows_total * width * hidden
        where = jnp.stack([lax.axis_index("dp"), lax.axis_index("tensor")]).astype(jnp.int32)
        scalars = (where, row_counts, segment_starts, owner_slot)
        (packed,) = call(
            pack_kernel,
            [((2 * SEG, wide), BF)],
            (),
            tuple(remote(x) for x in (hidden_in, tenant_basis, tenant_learned, tenant_bias)),
            scratch=[
                pltpu.VMEM(tenant_basis.shape, BF),
                pltpu.VMEM(tenant_learned.shape, BF),
                pltpu.VMEM(tenant_bias.shape, BF),
                pltpu.SemaphoreType.DMA((4,)),
            ],
            moved=4 * SEG * wide * 2,
            spec=pl.BlockSpec(memory_space=pl.ANY),
        )
        upstream_pieces = gather(grad_out)
        packed_pieces = gather(packed)
        marks = tuple(mark(x) for x in (packed, upstream_pieces[1], upstream_pieces[2]))
        upstream, back = call(
            functools.partial(back_kernel, n),
            [((rows_total, width), BF), ((rows_total, hidden), F32)],
            (),
            (*upstream_pieces, *marks, resident(down_weight)),
            flops=LONG_FLOPS,
            moved=2 * width * hidden,
            limit=n,
        )
        own, sent, scaled, rows, tables, middle, coeffs, stats = call(
            functools.partial(hidden_kernel, n, 1024),
            [
                ((SEG, width), F32),
                ((rows_total - SEG, width), BF),
                ((rows_total, width), F32),
                ((rows_total, wide), BF),
                ((rows_total, wide), BF),
                ((rows_total, width), BF),
                ((rows_total, rows_total), F32),
                ((rows_total, 128), F32),
            ],
            scalars,
            (
                *packed_pieces,
                norm_gain.reshape(1, width),
                back,
                resident(gate_weight),
                resident(up_weight),
            ),
            scratch=[
                pltpu.VMEM((rows_total, width), BF),
                pltpu.VMEM((rows_total, hidden), BF),
                pltpu.VMEM((rows_total, hidden), BF),
            ],
            flops=4 * work,
            moved=4 * width * hidden,
            limit=n + n // 2,
        )
        own_slot, sent_slot = call(
            functools.partial(slot_kernel, n, 512),
            [((SEG, wide), F32), ((rows_total - SEG, wide), BF)],
            scalars,
            (scaled, rows, tables, upstream, middle, coeffs, stats),
            scratch=[pltpu.VMEM((2, rows_total, width), BF)],
            flops=work,
            moved=10 * rows_total * width,
            limit=n + n // 2,
        )
        mine = reduce(own, sent)
        other = swap(mine)
        slots = reduce(own_slot, sent_slot)
        (grad_rows,) = call(
            functools.partial(rows_kernel, n),
            [((SEG, width), BF)],
            scalars,
            (mine, other, grad_out, middle, stats, tables),
            flops=LONG_FLOPS,
            moved=14 * SEG * width,
        )
        slots = slots + swap(slots)
        return (
            grad_rows,
            slots[None, :RANK, :width],
            slots[None, RANK:, :width],
            slots[None, RANK:, width],
        )

    return on_device


def solution(mesh):
    return jax.shard_map(
        make_device_function(mesh.shape["dp"]),
        mesh=mesh,
        in_specs=(
            P(("groups", "dp"), None),
            P(("groups", "dp"), None),
            P(),
            P(None, ("dp", "tensor")),
            P(None, ("dp", "tensor")),
            P(("dp", "tensor"), None),
            P(("groups", "dp"), None, None),
            P(("groups", "dp"), None, None),
            P(("groups", "dp"), None),
            P("groups"),
            P("groups"),
            P("groups"),
        ),
        out_specs=(
            P(("groups", "dp"), None),
            P(("groups", "dp"), None, None),
            P(("groups", "dp"), None, None),
            P(("groups", "dp"), None),
        ),
        check_vma=False,
    )
```

```python
import functools

import jax
import jax.numpy as jnp
from jax import lax
from jax.experimental import pallas as pl
from jax.experimental.pallas import tpu as pltpu
from jax.sharding import PartitionSpec as P

SEG = 16
RANK = 8
PAD = 128
EPS = 1e-05
BF = jnp.bfloat16
F32 = jnp.float32


def dot_nn(a, b):
    return jnp.dot(a, b, preferred_element_type=F32)


def dot_nt(a, b):
    return lax.dot_general(a, b, (((1,), (1,)), ((), ())), preferred_element_type=F32)


def split(x):
    high = x.astype(BF)
    low = (x - high.astype(F32)).astype(BF)
    return high, low


def ring_order(n):
    if n == 8:
        return [0, 2, 4, 6, 7, 5, 3, 1]
    return list(range(n))


def place_of(n, d):
    if n == 8:
        return jnp.where(d % 2 == 0, d // 2, n - 1 - d // 2)
    return d


def device_at(n, p):
    if n == 8:
        return jnp.where(p < n // 2, 2 * p, 2 * (n - 1 - p) + 1)
    return p


def piece_devices(n, where_ref):
    half = n // 2 - 1
    steps = [0] + [-t for t in range(1, half + 1)] + [t for t in range(1, half + 1)] + [n // 2]
    me = place_of(n, where_ref[0])
    sign = 1 - 2 * where_ref[1]
    return [device_at(n, lax.rem(me + sign * step + n, n)) for step in steps]


def block_tenant(device, counts_ref, starts_ref, slots_ref):
    first = device * SEG
    begin, count, slot = starts_ref[0], counts_ref[0], slots_ref[0]
    for t in range(1, starts_ref.shape[0]):
        reached = starts_ref[t] <= first
        begin = jnp.where(reached, starts_ref[t], begin)
        count = jnp.where(reached, counts_ref[t], count)
        slot = jnp.where(reached, slots_ref[t], slot)
    return slot, count - (first - begin)


def tenant_mask(n, where_ref, counts_ref, starts_ref, slots_ref):
    shape = (n * SEG, n * SEG)
    row = lax.broadcasted_iota(jnp.int32, shape, 0)
    column = lax.broadcasted_iota(jnp.int32, shape, 1)
    devices = piece_devices(n, where_ref)
    row_slot = jnp.zeros(shape, jnp.int32)
    row_limit = jnp.zeros(shape, jnp.int32)
    column_slot = jnp.zeros(shape, jnp.int32)
    for k, device in enumerate(devices):
        slot, limit = block_tenant(device, counts_ref, starts_ref, slots_ref)
        here = row // SEG == k
        row_slot = jnp.where(here, slot, row_slot)
        row_limit = jnp.where(here, limit, row_limit)
        column_slot = jnp.where(column // SEG == k, device, column_slot)
    keep = (row_slot == column_slot) & (row % SEG < row_limit) & (column % SEG < RANK)
    return jnp.where(keep, 1.0, 0.0)


def columns_at(c, step):
    return pl.ds(pl.multiple_of(c * step, step), step)


def pack_upstream_kernel(
    upstream_hbm, basis_hbm, learned_hbm, bias_hbm, packed_ref, basis_ref, learned_ref, bias_ref, sems
):
    width = upstream_hbm.shape[1]
    copies = (
        pltpu.make_async_copy(upstream_hbm, packed_ref.at[:, :width], sems.at[0]),
        pltpu.make_async_copy(basis_hbm, basis_ref, sems.at[1]),
        pltpu.make_async_copy(learned_hbm, learned_ref, sems.at[2]),
        pltpu.make_async_copy(bias_hbm, bias_ref, sems.at[3]),
    )
    for copy in copies:
        copy.start()
    for copy in copies:
        copy.wait()
    half = width // 2
    table = jnp.concatenate(
        [basis_ref[0, :, half:].astype(F32), learned_ref[0, :, half:].astype(F32)], axis=0
    )
    packed_ref[:, width : width + half] = table.astype(BF)
    shape = (SEG, PAD)
    row = lax.broadcasted_iota(jnp.int32, shape, 0)
    lane = lax.broadcasted_iota(jnp.int32, shape, 1)
    bias = jnp.zeros(shape, F32)
    wide = bias_ref[...].astype(F32)
    for r in range(RANK):
        bias = jnp.where((row == RANK + r) & (lane == 0), wide[:, r : r + 1], bias)
    packed_ref[:, width + half :] = bias.astype(BF)


def pack_rows_kernel(hidden_hbm, basis_hbm, learned_hbm, packed_ref, basis_ref, learned_ref, sems):
    width = hidden_hbm.shape[1]
    copies = (
        pltpu.make_async_copy(hidden_hbm, packed_ref.at[:, :width], sems.at[0]),
        pltpu.make_async_copy(basis_hbm, basis_ref, sems.at[1]),
        pltpu.make_async_copy(learned_hbm, learned_ref, sems.at[2]),
    )
    for copy in copies:
        copy.start()
    for copy in copies:
        copy.wait()
    lane = lax.broadcasted_iota(jnp.int32, (SEG, PAD), 1)
    packed_ref[:, width : width + PAD] = jnp.where(lane == 0, 1.0, 0.0).astype(BF)
    half = width // 2
    table = jnp.concatenate(
        [basis_ref[0, :, :half].astype(F32), learned_ref[0, :, :half].astype(F32)], axis=0
    )
    packed_ref[:, width + PAD :] = table.astype(BF)


def mark_kernel(after, out_ref):
    del after
    out_ref[...] = jnp.zeros_like(out_ref)


def back_kernel(n, *refs):
    pieces, (down_ref, upstream_ref, tables_ref, back_ref) = refs[:n], refs[-4:]
    width = upstream_ref.shape[1]
    for k, piece in enumerate(pieces):
        upstream_ref[k * SEG : (k + 1) * SEG, :] = piece[:, :width]
        tables_ref[k * SEG : (k + 1) * SEG, :] = piece[:, width:]
    back_ref[...] = dot_nt(upstream_ref[...], down_ref[...])


def hidden_kernel(n, step, *refs):
    where_ref, counts_ref, starts_ref, slots_ref = refs[:4]
    pieces = refs[4 : 4 + n]
    (
        gain_ref,
        back_ref,
        right_ref,
        gate_ref,
        up_ref,
        own_ref,
        sent_ref,
        scaled_ref,
        rows_ref,
        tables_ref,
        middle_ref,
        coeffs_ref,
        weights_ref,
        stats_ref,
        normed_ref,
        gate_grad_ref,
        up_grad_ref,
    ) = refs[4 + n :]
    row_total, width = middle_ref.shape
    chunks = width // step
    for k, piece in enumerate(pieces):
        rows_ref[k * SEG : (k + 1) * SEG, :] = piece[:, : width + PAD]
        tables_ref[k * SEG : (k + 1) * SEG, : width // 2] = piece[:, width + PAD :]
    tables_ref[:, width // 2 :] = right_ref[...]

    columns = tables_ref.shape[0]
    products = dot_nt(rows_ref[...], tables_ref[...])
    mask = tenant_mask(n, where_ref, counts_ref, starts_ref, slots_ref)
    coeffs = mask * (pltpu.roll(products, columns - RANK, 1) - products)
    coeffs_ref[...] = coeffs
    coeff_high, coeff_low = split(coeffs)

    def middle_step(c, carry):
        squares, middle_tables = carry
        cols = columns_at(c, step)
        table = tables_ref[:, cols]
        value = rows_ref[:, cols].astype(F32) + (
            dot_nn(coeff_high, table) + dot_nn(coeff_low, table)
        )
        value = value.astype(BF)
        middle_ref[:, cols] = value
        middle_tables = middle_tables + dot_nt(value, table)
        value = value.astype(F32)
        return squares + jnp.sum(value * value, axis=1, keepdims=True), middle_tables

    column_zero = jnp.zeros((row_total, 1), F32)
    square_zero = jnp.zeros((row_total, columns), F32)
    squares, middle_tables = lax.fori_loop(0, chunks, middle_step, (column_zero, square_zero))
    inverse = lax.rsqrt(squares / width + EPS)

    def normed_step(c, carry):
        cols = columns_at(c, step)
        value = middle_ref[:, cols].astype(F32) * inverse * gain_ref[:, cols]
        normed_ref[:, cols] = value.astype(BF)
        return carry

    lax.fori_loop(0, chunks, normed_step, 0)

    hidden = gate_ref.shape[1]
    tile = min(256, hidden)
    for j in range(hidden // tile):
        cols = slice(j * tile, (j + 1) * tile)
        gate = dot_nn(normed_ref[...], gate_ref[:, cols])
        upward = dot_nn(normed_ref[...], up_ref[:, cols])
        back = back_ref[:, cols]
        sigma = jax.nn.sigmoid(gate)
        gate_grad_ref[:, cols] = (back * upward * sigma * (1.0 + gate * (1.0 - sigma))).astype(BF)
        up_grad_ref[:, cols] = (back * gate * sigma).astype(BF)

    def scaled_step(c, carry):
        inner, scaled_tables = carry
        cols = columns_at(c, step)
        value = dot_nt(gate_grad_ref[...], gate_ref[cols, :])
        value = value + dot_nt(up_grad_ref[...], up_ref[cols, :])
        value = value * gain_ref[:, cols]
        scaled_ref[:, cols] = value
        own_ref[:, cols] = value[:SEG]
        high = value.astype(BF)
        sent_ref[:, cols] = high[SEG:]
        scaled_tables = scaled_tables + dot_nt(high, tables_ref[:, cols])
        inner = inner + jnp.sum(value * middle_ref[:, cols].astype(F32), axis=1, keepdims=True)
        return inner, scaled_tables

    inner, scaled_tables = lax.fori_loop(0, chunks, scaled_step, (column_zero, square_zero))
    shrink = inverse * inverse * (inner / width)
    lane = lax.broadcasted_iota(jnp.int32, stats_ref.shape, 1)
    stats_ref[...] = jnp.where(lane == 0, inverse, shrink)
    pulled = mask * (inverse * (scaled_tables - shrink * middle_tables))
    pulled = pltpu.roll(pulled, RANK, 1) - pulled
    weights_ref[:, :row_total] = coeffs.T.astype(BF)
    weights_ref[:, row_total:] = pulled.T.astype(BF)


def slot_kernel(
    step,
    scaled_ref,
    rows_ref,
    middle_ref,
    weights_ref,
    stats_ref,
    own_ref,
    sent_ref,
):
    row_total, width = middle_ref.shape
    inverse, shrink = stats_ref[:, 0:1], stats_ref[:, 1:2]

    def slot_step(c, carry):
        cols = columns_at(c, step)
        value = inverse * (scaled_ref[:, cols] - middle_ref[:, cols].astype(F32) * shrink)
        both = jnp.concatenate([value.astype(BF), rows_ref[:, cols]], axis=0)
        value = dot_nn(weights_ref[...], both)
        sent_ref[:, cols] = value[SEG:].astype(BF)
        own_ref[:, cols] = value[:SEG]
        return carry

    lax.fori_loop(0, width // step, slot_step, 0)
    value = dot_nn(weights_ref[:, row_total:], rows_ref[:, width:])
    sent_ref[:, width:] = value[SEG:].astype(BF)
    own_ref[:, width:] = value[:SEG]


def local_kernel(
    n,
    step,
    where_ref,
    counts_ref,
    starts_ref,
    slots_ref,
    rows_ref,
    tables_ref,
    upstream_ref,
    coeffs_ref,
    local_ref,
):
    row_total, width = upstream_ref.shape
    columns = tables_ref.shape[0]
    mask = tenant_mask(n, where_ref, counts_ref, starts_ref, slots_ref)
    lane = lax.broadcasted_iota(jnp.int32, (row_total, columns), 1)
    first = lane < RANK
    pulled = jnp.where(first, mask, 0.0) * dot_nt(upstream_ref[...], tables_ref[:, :width])
    pulled = pltpu.roll(pulled, RANK, 1) - pulled
    coeffs = jnp.where(first, coeffs_ref[...], 0.0)
    coeff_high, coeff_low = split(coeffs.T[:SEG])
    pulled_high, pulled_low = split(pulled.T[:SEG])

    def local_step(c, carry):
        cols = columns_at(c, step)
        upstream, rows = upstream_ref[:, cols], rows_ref[:, cols]
        value = dot_nn(coeff_high, upstream) + dot_nn(coeff_low, upstream)
        local_ref[:, cols] = value + (dot_nn(pulled_high, rows) + dot_nn(pulled_low, rows))
        return carry

    lax.fori_loop(0, width // step, local_step, 0)
    rows = rows_ref[:, width:]
    local_ref[:, width:] = dot_nn(pulled_high, rows) + dot_nn(pulled_low, rows)


def ends_kernel(mine_ref, other_ref, local_ref, after, basis_ref, learned_ref, bias_ref):
    del after
    width = basis_ref.shape[2]
    value = mine_ref[...] + other_ref[...] + local_ref[...]
    basis_ref[0, :, :] = value[:RANK, :width]
    learned_ref[0, :, :] = value[RANK:, :width]
    row = lax.broadcasted_iota(jnp.int32, (RANK, RANK), 0)
    lane = lax.broadcasted_iota(jnp.int32, (RANK, RANK), 1)
    bias = jnp.where(row == lane, value[RANK:, width : width + 1], 0.0)
    bias_ref[...] = jnp.sum(bias, axis=0, keepdims=True)


def rows_kernel(
    n,
    where_ref,
    counts_ref,
    starts_ref,
    slots_ref,
    mine_ref,
    other_ref,
    upstream_ref,
    middle_ref,
    stats_ref,
    tables_ref,
    out_ref,
):
    width = out_ref.shape[1]
    devices = piece_devices(n, where_ref)
    slot, limit = block_tenant(devices[0], counts_ref, starts_ref, slots_ref)
    which = 0
    for k, device in enumerate(devices):
        which = jnp.where(device == slot, k, which)
    table = tables_ref[pl.ds(pl.multiple_of(which * SEG, SEG), SEG), :width]
    middle = middle_ref[:SEG, :].astype(F32)
    inverse = stats_ref[:SEG, 0:1]
    scaled = mine_ref[...] + other_ref[...]
    inner = jnp.sum(scaled * middle, axis=1, keepdims=True) / width
    total = upstream_ref[...].astype(F32) + inverse * (
        scaled - middle * (inverse * inverse * inner)
    )
    high, low = split(total)
    pulled = dot_nt(high, table) + dot_nt(low, table)
    row = lax.broadcasted_iota(jnp.int32, (SEG, RANK), 0)
    pulled = jnp.where(row < limit, pulled[:, :RANK], 0.0)
    pulled = jnp.concatenate([-pulled, pulled], axis=1)
    high, low = split(pulled)
    out_ref[...] = (total + dot_nn(high, table) + dot_nn(low, table)).astype(BF)


LOAD_FLOPS = 4 * 10**9
LONG_FLOPS = 40 * 10**9
SMEM_SPEC = pl.BlockSpec(memory_space=pltpu.SMEM)
VMEM_SPEC = pl.BlockSpec(memory_space=pltpu.VMEM)
ANY_SPEC = pl.BlockSpec(memory_space=pl.ANY)


def call(kernel, outs, scalars, arrays, scratch=(), flops=0, moved=0, limit=4, spec=None, loose=0):
    return pl.pallas_call(
        kernel,
        out_shape=tuple(jax.ShapeDtypeStruct(s, d) for s, d in outs),
        in_specs=[SMEM_SPEC] * len(scalars)
        + [spec or VMEM_SPEC] * (len(arrays) - loose)
        + [ANY_SPEC] * loose,
        out_specs=tuple(VMEM_SPEC for _ in outs),
        scratch_shapes=list(scratch),
        compiler_params=pltpu.CompilerParams(vmem_limit_bytes=limit * 1024 * 1024),
        cost_estimate=pl.CostEstimate(flops=flops, bytes_accessed=moved, transcendentals=0),
    )(*scalars, *arrays)


def resident(x):
    return pltpu.with_memory_space_constraint(x, pltpu.VMEM)


def remote(x):
    return pltpu.with_memory_space_constraint(x, pltpu.HBM)


def mark(after):
    (out,) = call(
        mark_kernel, [((8, 128), F32)], (), (after,), flops=LOAD_FLOPS, spec=pl.BlockSpec(memory_space=pl.ANY)
    )
    return out


def make_device_function(n):
    order = ring_order(n)
    place = {d: k for k, d in enumerate(order)}
    half = n // 2 - 1
    pairs = []
    for d in range(n):
        pairs.append((d * 2, order[(place[d] + 1) % n] * 2))
        pairs.append((d * 2 + 1, order[(place[d] - 1) % n] * 2 + 1))

    def hop(x):
        return lax.ppermute(x, ("dp", "tensor"), pairs)

    def swap(x):
        return lax.ppermute(x, "tensor", [(0, 1), (1, 0)])

    def gather(x):
        ahead, behind = [], []
        state = x
        for _ in range(half):
            state = hop(state)
            ahead.append(state)
            behind.append(swap(state))
        return [x] + ahead + behind + [hop(state)]

    def reduce(own, sent):
        other = swap(sent[: half * SEG])
        state = hop(sent[2 * half * SEG :])
        for t in range(half - 1, -1, -1):
            mine = sent[(half + t) * SEG : (half + t + 1) * SEG].astype(F32)
            partner = other[t * SEG : (t + 1) * SEG].astype(F32)
            state = hop((state.astype(F32) + (mine + partner)).astype(BF))
        return own + state.astype(F32)

    def on_device(
        hidden_in,
        grad_out,
        norm_gain,
        gate_weight,
        up_weight,
        down_weight,
        tenant_basis,
        tenant_learned,
        tenant_bias,
        row_counts,
        segment_starts,
        owner_slot,
    ):
        width = hidden_in.shape[1]
        hidden = gate_weight.shape[1]
        wide = width + PAD
        rows_total = n * SEG
        work = 2 * rows_total * width * hidden
        where = jnp.stack([lax.axis_index("dp"), lax.axis_index("tensor")]).astype(jnp.int32)
        scalars = (where, row_counts, segment_starts, owner_slot)
        tables_scratch = [
            pltpu.VMEM(tenant_basis.shape, BF),
            pltpu.VMEM(tenant_learned.shape, BF),
        ]
        hbm = pl.BlockSpec(memory_space=pltpu.MemorySpace.HBM)
        (packed_upstream,) = call(
            pack_upstream_kernel,
            [((SEG, width + width // 2 + PAD), BF)],
            (),
            tuple(remote(x) for x in (grad_out, tenant_basis, tenant_learned, tenant_bias)),
            scratch=tables_scratch
            + [pltpu.VMEM(tenant_bias.shape, BF), pltpu.SemaphoreType.DMA((4,))],
            moved=4 * SEG * wide * 2,
            spec=hbm,
        )
        (packed_rows,) = call(
            pack_rows_kernel,
            [((SEG, width + width // 2 + PAD), BF)],
            (),
            tuple(remote(x) for x in (hidden_in, tenant_basis, tenant_learned)),
            scratch=tables_scratch + [pltpu.SemaphoreType.DMA((3,))],
            moved=4 * SEG * wide * 2,
            spec=hbm,
        )
        upstream_pieces = gather(packed_upstream)
        row_pieces = gather(packed_rows)
        marks = tuple(mark(x) for x in (packed_rows, upstream_pieces[1], upstream_pieces[2]))
        upstream, right, back = call(
            functools.partial(back_kernel, n),
            [
                ((rows_total, width), BF),
                ((rows_total, width // 2 + PAD), BF),
                ((rows_total, hidden), F32),
            ],
            (),
            (*upstream_pieces, *marks, resident(down_weight)),
            flops=LONG_FLOPS,
            moved=2 * width * hidden,
            limit=n,
        )
        own, sent, scaled, rows, tables, middle, coeffs, weights, stats = call(
            functools.partial(hidden_kernel, n, 1024),
            [
                ((SEG, width), F32),
                ((rows_total - SEG, width), BF),
                ((rows_total, width), F32),
                ((rows_total, wide), BF),
                ((rows_total, wide), BF),
                ((rows_total, width), BF),
                ((rows_total, rows_total), F32),
                ((rows_total, 2 * rows_total), BF),
                ((rows_total, 128), F32),
            ],
            scalars,
            (
                *row_pieces,
                norm_gain.reshape(1, width),
                back,
                right,
                resident(gate_weight),
                resident(up_weight),
            ),
            scratch=[
                pltpu.VMEM((rows_total, width), BF),
                pltpu.VMEM((rows_total, hidden), BF),
                pltpu.VMEM((rows_total, hidden), BF),
            ],
            flops=4 * work,
            moved=4 * width * hidden,
            limit=n + n // 2,
        )
        own_slot, sent_slot = call(
            functools.partial(slot_kernel, 1024),
            [((SEG, wide), F32), ((rows_total - SEG, wide), BF)],
            (),
            (scaled, rows, middle, weights, stats),
            flops=work,
            moved=10 * rows_total * width,
            limit=n + n // 2,
        )
        (local,) = call(
            functools.partial(local_kernel, n, 1024),
            [((SEG, wide), F32)],
            scalars,
            (rows, tables, upstream, coeffs),
            flops=work,
            moved=10 * rows_total * width,
            limit=n + n // 2,
        )
        mine = reduce(own, sent)
        other = swap(mine)
        slots = reduce(own_slot, sent_slot)
        (grad_rows,) = call(
            functools.partial(rows_kernel, n),
            [((SEG, width), BF)],
            scalars,
            (mine, other, grad_out, middle, stats, tables),
            flops=LONG_FLOPS,
            moved=14 * SEG * width,
        )
        outs = call(
            ends_kernel,
            [((1, RANK, width), F32), ((1, RANK, width), F32), ((1, RANK), F32)],
            (),
            (slots, swap(slots), local, grad_rows),
            moved=20 * SEG * width,
            loose=1,
        )
        return (grad_rows, *outs)

    return on_device


def solution(mesh):
    return jax.shard_map(
        make_device_function(mesh.shape["dp"]),
        mesh=mesh,
        in_specs=(
            P(("groups", "dp"), None),
            P(("groups", "dp"), None),
            P(),
            P(None, ("dp", "tensor")),
            P(None, ("dp", "tensor")),
            P(("dp", "tensor"), None),
            P(("groups", "dp"), None, None),
            P(("groups", "dp"), None, None),
            P(("groups", "dp"), None),
            P("groups"),
            P("groups"),
            P("groups"),
        ),
        out_specs=(
            P(("groups", "dp"), None),
            P(("groups", "dp"), None, None),
            P(("groups", "dp"), None, None),
            P(("groups", "dp"), None),
        ),
        check_vma=False,
    )
```

```python
import functools

import jax
import jax.numpy as jnp
from jax import lax
from jax.experimental import pallas as pl
from jax.experimental.pallas import tpu as pltpu
from jax.sharding import PartitionSpec as P

SEG = 16
RANK = 8
PAD = 128
EPS = 1e-05
BF = jnp.bfloat16
F32 = jnp.float32


def dot_nn(a, b):
    return jnp.dot(a, b, preferred_element_type=F32)


def dot_nt(a, b):
    return lax.dot_general(a, b, (((1,), (1,)), ((), ())), preferred_element_type=F32)


def split(x):
    high = x.astype(BF)
    low = (x - high.astype(F32)).astype(BF)
    return high, low


def ring_order(n):
    if n == 8:
        return [0, 2, 4, 6, 7, 5, 3, 1]
    return list(range(n))


def place_of(n, d):
    if n == 8:
        return jnp.where(d % 2 == 0, d // 2, n - 1 - d // 2)
    return d


def device_at(n, p):
    if n == 8:
        return jnp.where(p < n // 2, 2 * p, 2 * (n - 1 - p) + 1)
    return p


def piece_devices(n, where_ref):
    half = n // 2 - 1
    steps = [0] + [-t for t in range(1, half + 1)] + [t for t in range(1, half + 1)] + [n // 2]
    me = place_of(n, where_ref[0])
    sign = 1 - 2 * where_ref[1]
    return [device_at(n, lax.rem(me + sign * step + n, n)) for step in steps]


def block_tenant(device, counts_ref, starts_ref, slots_ref):
    first = device * SEG
    begin, count, slot = starts_ref[0], counts_ref[0], slots_ref[0]
    for t in range(1, starts_ref.shape[0]):
        reached = starts_ref[t] <= first
        begin = jnp.where(reached, starts_ref[t], begin)
        count = jnp.where(reached, counts_ref[t], count)
        slot = jnp.where(reached, slots_ref[t], slot)
    return slot, count - (first - begin)


def tenant_mask(n, where_ref, counts_ref, starts_ref, slots_ref):
    shape = (n * SEG, n * SEG)
    row = lax.broadcasted_iota(jnp.int32, shape, 0)
    column = lax.broadcasted_iota(jnp.int32, shape, 1)
    devices = piece_devices(n, where_ref)
    row_slot = jnp.zeros(shape, jnp.int32)
    row_limit = jnp.zeros(shape, jnp.int32)
    column_slot = jnp.zeros(shape, jnp.int32)
    for k, device in enumerate(devices):
        slot, limit = block_tenant(device, counts_ref, starts_ref, slots_ref)
        here = row // SEG == k
        row_slot = jnp.where(here, slot, row_slot)
        row_limit = jnp.where(here, limit, row_limit)
        column_slot = jnp.where(column // SEG == k, device, column_slot)
    keep = (row_slot == column_slot) & (row % SEG < row_limit) & (column % SEG < RANK)
    return jnp.where(keep, 1.0, 0.0)


def columns_at(c, step):
    return pl.ds(pl.multiple_of(c * step, step), step)


def pack_upstream_kernel(
    upstream_hbm, basis_hbm, learned_hbm, bias_hbm, packed_ref, basis_ref, learned_ref, bias_ref, sems
):
    width = upstream_hbm.shape[1]
    copies = (
        pltpu.make_async_copy(upstream_hbm, packed_ref.at[:, :width], sems.at[0]),
        pltpu.make_async_copy(basis_hbm, basis_ref, sems.at[1]),
        pltpu.make_async_copy(learned_hbm, learned_ref, sems.at[2]),
        pltpu.make_async_copy(bias_hbm, bias_ref, sems.at[3]),
    )
    for copy in copies:
        copy.start()
    for copy in copies:
        copy.wait()
    half = width // 2
    table = jnp.concatenate(
        [basis_ref[0, :, half:].astype(F32), learned_ref[0, :, half:].astype(F32)], axis=0
    )
    packed_ref[:, width : width + half] = table.astype(BF)
    shape = (SEG, PAD)
    row = lax.broadcasted_iota(jnp.int32, shape, 0)
    lane = lax.broadcasted_iota(jnp.int32, shape, 1)
    bias = jnp.zeros(shape, F32)
    wide = bias_ref[...].astype(F32)
    for r in range(RANK):
        bias = jnp.where((row == RANK + r) & (lane == 0), wide[:, r : r + 1], bias)
    packed_ref[:, width + half :] = bias.astype(BF)


def pack_rows_kernel(hidden_hbm, basis_hbm, learned_hbm, packed_ref, basis_ref, learned_ref, sems):
    width = hidden_hbm.shape[1]
    copies = (
        pltpu.make_async_copy(hidden_hbm, packed_ref.at[:, :width], sems.at[0]),
        pltpu.make_async_copy(basis_hbm, basis_ref, sems.at[1]),
        pltpu.make_async_copy(learned_hbm, learned_ref, sems.at[2]),
    )
    for copy in copies:
        copy.start()
    for copy in copies:
        copy.wait()
    lane = lax.broadcasted_iota(jnp.int32, (SEG, PAD), 1)
    packed_ref[:, width : width + PAD] = jnp.where(lane == 0, 1.0, 0.0).astype(BF)
    half = width // 2
    table = jnp.concatenate(
        [basis_ref[0, :, :half].astype(F32), learned_ref[0, :, :half].astype(F32)], axis=0
    )
    packed_ref[:, width + PAD :] = table.astype(BF)


def mark_kernel(after, out_ref):
    del after
    out_ref[...] = jnp.zeros_like(out_ref)


def mask_kernel(n, where_ref, counts_ref, starts_ref, slots_ref, after, mask_ref):
    del after
    mask_ref[...] = tenant_mask(n, where_ref, counts_ref, starts_ref, slots_ref)


def back_kernel(n, *refs):
    pieces, (down_ref, upstream_ref, tables_ref, back_ref) = refs[:n], refs[-4:]
    width = upstream_ref.shape[1]
    for k, piece in enumerate(pieces):
        upstream_ref[k * SEG : (k + 1) * SEG, :] = piece[:, :width]
        tables_ref[k * SEG : (k + 1) * SEG, :] = piece[:, width:]
    back_ref[...] = dot_nt(upstream_ref[...], down_ref[...])


def hidden_kernel(n, step, *refs):
    pieces = refs[:n]
    (
        mask_ref,
        gain_ref,
        back_ref,
        right_ref,
        gate_ref,
        up_ref,
        own_ref,
        sent_ref,
        scaled_ref,
        rows_ref,
        tables_ref,
        middle_ref,
        coeffs_ref,
        pulled_ref,
        stats_ref,
        normed_ref,
        gate_t_ref,
        gate_grad_ref,
        up_grad_ref,
    ) = refs[n:]
    row_total, width = middle_ref.shape
    chunks = width // step
    for k, piece in enumerate(pieces):
        rows_ref[k * SEG : (k + 1) * SEG, :] = piece[:, : width + PAD]
        tables_ref[k * SEG : (k + 1) * SEG, : width // 2] = piece[:, width + PAD :]
    tables_ref[:, width // 2 :] = right_ref[...]

    columns = tables_ref.shape[0]
    products = dot_nt(rows_ref[...], tables_ref[...])
    mask = mask_ref[...]
    coeffs = mask * (pltpu.roll(products, columns - RANK, 1) - products)
    coeffs_ref[...] = coeffs
    coeff_high, coeff_low = split(coeffs)

    def middle_step(c, carry):
        squares, middle_tables = carry
        cols = columns_at(c, step)
        table = tables_ref[:, cols]
        value = rows_ref[:, cols].astype(F32) + (
            dot_nn(coeff_high, table) + dot_nn(coeff_low, table)
        )
        value = value.astype(BF)
        middle_ref[:, cols] = value
        middle_tables = middle_tables + dot_nt(value, table)
        value = value.astype(F32)
        return squares + jnp.sum(value * value, axis=1, keepdims=True), middle_tables

    column_zero = jnp.zeros((row_total, 1), F32)
    square_zero = jnp.zeros((row_total, columns), F32)
    squares, middle_tables = lax.fori_loop(0, chunks, middle_step, (column_zero, square_zero))
    inverse = lax.rsqrt(squares / width + EPS)

    def normed_step(c, carry):
        cols = columns_at(c, step)
        value = middle_ref[:, cols].astype(F32) * inverse * gain_ref[:, cols]
        normed_ref[:, cols] = value.astype(BF)
        return carry

    lax.fori_loop(0, chunks, normed_step, 0)

    hidden = gate_ref.shape[1]
    tile = min(256, hidden)
    for j in range(hidden // tile):
        cols = slice(j * tile, (j + 1) * tile)
        gate = dot_nn(normed_ref[...], gate_ref[:, cols])
        gate_t_ref[cols, :] = gate_ref[:, cols].T
        upward = dot_nn(normed_ref[...], up_ref[:, cols])
        back = back_ref[:, cols]
        sigma = jax.nn.sigmoid(gate)
        gate_grad_ref[:, cols] = (back * upward * sigma * (1.0 + gate * (1.0 - sigma))).astype(BF)
        up_grad_ref[:, cols] = (back * gate * sigma).astype(BF)

    inner, scaled_tables = column_zero, square_zero
    for c in range(chunks):
        cols = slice(c * step, (c + 1) * step)
        value = dot_nn(gate_grad_ref[...], gate_t_ref[:, cols])
        value = value + dot_nt(up_grad_ref[...], up_ref[cols, :])
        value = value * gain_ref[:, cols]
        scaled_ref[:, cols] = value
        own_ref[:, cols] = value[:SEG]
        high = value.astype(BF)
        sent_ref[:, cols] = high[SEG:]
        scaled_tables = scaled_tables + dot_nt(high, tables_ref[:, cols])
        inner = inner + jnp.sum(value * middle_ref[:, cols].astype(F32), axis=1, keepdims=True)

    shrink = inverse * inverse * (inner / width)
    lane = lax.broadcasted_iota(jnp.int32, stats_ref.shape, 1)
    stats_ref[...] = jnp.where(lane == 0, inverse, shrink)
    pulled_ref[...] = mask * (inverse * (scaled_tables - shrink * middle_tables))


def slot_kernel(
    step,
    scaled_ref,
    rows_ref,
    middle_ref,
    coeffs_ref,
    pulled_ref,
    stats_ref,
    own_ref,
    sent_ref,
    weights_ref,
):
    row_total, width = middle_ref.shape
    inverse, shrink = stats_ref[:, 0:1], stats_ref[:, 1:2]
    pulled = pulled_ref[...]
    pulled = pltpu.roll(pulled, RANK, 1) - pulled
    weights_ref[:, :row_total] = coeffs_ref[...].T.astype(BF)
    weights_ref[:, row_total:] = pulled.T.astype(BF)

    for c in range(width // step):
        cols = slice(c * step, (c + 1) * step)
        value = inverse * (scaled_ref[:, cols] - middle_ref[:, cols].astype(F32) * shrink)
        both = jnp.concatenate([value.astype(BF), rows_ref[:, cols]], axis=0)
        value = dot_nn(weights_ref[...], both)
        sent_ref[:, cols] = value[SEG:].astype(BF)
        own_ref[:, cols] = value[:SEG]
    value = dot_nn(weights_ref[:, row_total:], rows_ref[:, width:])
    sent_ref[:, width:] = value[SEG:].astype(BF)
    own_ref[:, width:] = value[:SEG]


def local_kernel(step, mask_ref, rows_ref, tables_ref, upstream_ref, coeffs_ref, after, local_ref):
    del after
    row_total, width = upstream_ref.shape
    columns = tables_ref.shape[0]
    mask = mask_ref[...]
    lane = lax.broadcasted_iota(jnp.int32, (row_total, columns), 1)
    first = lane < RANK
    pulled = jnp.where(first, mask, 0.0) * dot_nt(upstream_ref[...], tables_ref[:, :width])
    pulled = pltpu.roll(pulled, RANK, 1) - pulled
    coeffs = jnp.where(first, coeffs_ref[...], 0.0)
    coeff_high, coeff_low = split(coeffs.T[:SEG])
    pulled_high, pulled_low = split(pulled.T[:SEG])

    def local_step(c, carry):
        cols = columns_at(c, step)
        upstream, rows = upstream_ref[:, cols], rows_ref[:, cols]
        value = dot_nn(coeff_high, upstream) + dot_nn(coeff_low, upstream)
        local_ref[:, cols] = value + (dot_nn(pulled_high, rows) + dot_nn(pulled_low, rows))
        return carry

    lax.fori_loop(0, width // step, local_step, 0)
    rows = rows_ref[:, width:]
    local_ref[:, width:] = dot_nn(pulled_high, rows) + dot_nn(pulled_low, rows)


def ends_kernel(mine_ref, other_ref, local_ref, after, basis_ref, learned_ref, bias_ref):
    del after
    width = basis_ref.shape[2]
    value = mine_ref[...] + other_ref[...] + local_ref[...]
    basis_ref[0, :, :] = value[:RANK, :width]
    learned_ref[0, :, :] = value[RANK:, :width]
    row = lax.broadcasted_iota(jnp.int32, (RANK, RANK), 0)
    lane = lax.broadcasted_iota(jnp.int32, (RANK, RANK), 1)
    bias = jnp.where(row == lane, value[RANK:, width : width + 1], 0.0)
    bias_ref[...] = jnp.sum(bias, axis=0, keepdims=True)


def rows_kernel(
    n,
    where_ref,
    counts_ref,
    starts_ref,
    slots_ref,
    mine_ref,
    other_ref,
    upstream_ref,
    middle_ref,
    stats_ref,
    tables_ref,
    out_ref,
    token_ref,
):
    width = out_ref.shape[1]
    token_ref[...] = jnp.zeros_like(token_ref)
    devices = piece_devices(n, where_ref)
    slot, limit = block_tenant(devices[0], counts_ref, starts_ref, slots_ref)
    which = 0
    for k, device in enumerate(devices):
        which = jnp.where(device == slot, k, which)
    table = tables_ref[pl.ds(pl.multiple_of(which * SEG, SEG), SEG), :width]
    middle = middle_ref[:SEG, :].astype(F32)
    inverse = stats_ref[:SEG, 0:1]
    scaled = mine_ref[...] + other_ref[...]
    inner = jnp.sum(scaled * middle, axis=1, keepdims=True) / width
    total = upstream_ref[:SEG, :].astype(F32) + inverse * (
        scaled - middle * (inverse * inverse * inner)
    )
    pulled = dot_nt(total.astype(BF), table)
    row = lax.broadcasted_iota(jnp.int32, (SEG, RANK), 0)
    pulled = jnp.where(row < limit, pulled[:, :RANK], 0.0)
    pulled = jnp.concatenate([-pulled, pulled], axis=1).astype(BF)
    out_ref[...] = (total + dot_nn(pulled, table)).astype(BF)


LOAD_FLOPS = 4 * 10**9
LONG_FLOPS = 40 * 10**9
SMEM_SPEC = pl.BlockSpec(memory_space=pltpu.SMEM)
VMEM_SPEC = pl.BlockSpec(memory_space=pltpu.VMEM)
ANY_SPEC = pl.BlockSpec(memory_space=pl.ANY)


def call(kernel, outs, scalars, arrays, scratch=(), flops=0, moved=0, limit=4, spec=None, loose=0):
    return pl.pallas_call(
        kernel,
        out_shape=tuple(jax.ShapeDtypeStruct(s, d) for s, d in outs),
        in_specs=[SMEM_SPEC] * len(scalars)
        + [spec or VMEM_SPEC] * (len(arrays) - loose)
        + [ANY_SPEC] * loose,
        out_specs=tuple(VMEM_SPEC for _ in outs),
        scratch_shapes=list(scratch),
        compiler_params=pltpu.CompilerParams(vmem_limit_bytes=limit * 1024 * 1024),
        cost_estimate=pl.CostEstimate(flops=flops, bytes_accessed=moved, transcendentals=0),
    )(*scalars, *arrays)


def resident(x):
    return pltpu.with_memory_space_constraint(x, pltpu.VMEM)


def remote(x):
    return pltpu.with_memory_space_constraint(x, pltpu.HBM)


def mark(after):
    (out,) = call(
        mark_kernel, [((8, 128), F32)], (), (after,), flops=LOAD_FLOPS, spec=pl.BlockSpec(memory_space=pl.ANY)
    )
    return out


def make_device_function(n):
    order = ring_order(n)
    place = {d: k for k, d in enumerate(order)}
    half = n // 2 - 1
    pairs = []
    for d in range(n):
        pairs.append((d * 2, order[(place[d] + 1) % n] * 2))
        pairs.append((d * 2 + 1, order[(place[d] - 1) % n] * 2 + 1))

    def hop(x):
        return lax.ppermute(x, ("dp", "tensor"), pairs)

    def swap(x):
        return lax.ppermute(x, "tensor", [(0, 1), (1, 0)])

    def gather(x):
        ahead, behind = [], []
        state = x
        for _ in range(half):
            state = hop(state)
            ahead.append(state)
            behind.append(swap(state))
        return [x] + ahead + behind + [hop(state)]

    def reduce(own, sent):
        other = swap(sent[: half * SEG])
        state = hop(sent[2 * half * SEG :])
        states = [state]
        for t in range(half - 1, -1, -1):
            mine = sent[(half + t) * SEG : (half + t + 1) * SEG].astype(F32)
            partner = other[t * SEG : (t + 1) * SEG].astype(F32)
            state = hop((state.astype(F32) + (mine + partner)).astype(BF))
            states.append(state)
        return own + state.astype(F32), states

    def on_device(
        hidden_in,
        grad_out,
        norm_gain,
        gate_weight,
        up_weight,
        down_weight,
        tenant_basis,
        tenant_learned,
        tenant_bias,
        row_counts,
        segment_starts,
        owner_slot,
    ):
        width = hidden_in.shape[1]
        hidden = gate_weight.shape[1]
        wide = width + PAD
        rows_total = n * SEG
        work = 2 * rows_total * width * hidden
        where = jnp.stack([lax.axis_index("dp"), lax.axis_index("tensor")]).astype(jnp.int32)
        scalars = (where, row_counts, segment_starts, owner_slot)
        tables_scratch = [
            pltpu.VMEM(tenant_basis.shape, BF),
            pltpu.VMEM(tenant_learned.shape, BF),
        ]
        hbm = pl.BlockSpec(memory_space=pltpu.MemorySpace.HBM)
        (packed_upstream,) = call(
            pack_upstream_kernel,
            [((SEG, width + width // 2 + PAD), BF)],
            (),
            tuple(remote(x) for x in (grad_out, tenant_basis, tenant_learned, tenant_bias)),
            scratch=tables_scratch
            + [pltpu.VMEM(tenant_bias.shape, BF), pltpu.SemaphoreType.DMA((4,))],
            moved=4 * SEG * wide * 2,
            spec=hbm,
        )
        (packed_rows,) = call(
            pack_rows_kernel,
            [((SEG, width + width // 2 + PAD), BF)],
            (),
            tuple(remote(x) for x in (hidden_in, tenant_basis, tenant_learned)),
            scratch=tables_scratch + [pltpu.SemaphoreType.DMA((3,))],
            moved=4 * SEG * wide * 2,
            spec=hbm,
        )
        upstream_pieces = gather(packed_upstream)
        row_pieces = gather(packed_rows)
        marks = tuple(mark(x) for x in (packed_rows, upstream_pieces[2]))
        (mask,) = call(
            functools.partial(mask_kernel, n),
            [((rows_total, rows_total), F32)],
            scalars,
            (upstream_pieces[1],),
            flops=LOAD_FLOPS,
            loose=1,
            limit=max(4, n // 2),
        )
        upstream, right, back = call(
            functools.partial(back_kernel, n),
            [
                ((rows_total, width), BF),
                ((rows_total, width // 2 + PAD), BF),
                ((rows_total, hidden), F32),
            ],
            (),
            (*upstream_pieces, *marks, resident(down_weight)),
            flops=LONG_FLOPS,
            moved=2 * width * hidden,
            limit=n,
        )
        own, sent, scaled, rows, tables, middle, coeffs, pulled, stats = call(
            functools.partial(hidden_kernel, n, 1024),
            [
                ((SEG, width), F32),
                ((rows_total - SEG, width), BF),
                ((rows_total, width), F32),
                ((rows_total, wide), BF),
                ((rows_total, wide), BF),
                ((rows_total, width), BF),
                ((rows_total, rows_total), F32),
                ((rows_total, rows_total), F32),
                ((rows_total, 128), F32),
            ],
            (),
            (
                *row_pieces,
                mask,
                norm_gain.reshape(1, width),
                back,
                right,
                resident(gate_weight),
                resident(up_weight),
            ),
            scratch=[
                pltpu.VMEM((rows_total, width), BF),
                pltpu.VMEM((hidden, width), BF),
                pltpu.VMEM((rows_total, hidden), BF),
                pltpu.VMEM((rows_total, hidden), BF),
            ],
            flops=4 * work,
            moved=4 * width * hidden,
            limit=n + n // 2 + 8,
        )
        own_slot, sent_slot = call(
            functools.partial(slot_kernel, 1024),
            [((SEG, wide), F32), ((rows_total - SEG, wide), BF)],
            (),
            (scaled, rows, middle, coeffs, pulled, stats),
            scratch=[pltpu.VMEM((rows_total, 2 * rows_total), BF)],
            flops=work,
            moved=10 * rows_total * width,
            limit=n + n // 2,
        )
        mine, states = reduce(own, sent)
        other = swap(mine)
        slots, _ = reduce(own_slot, sent_slot)
        (local,) = call(
            functools.partial(local_kernel, 1024),
            [((SEG, wide), F32)],
            (),
            (mask, rows, tables, upstream, coeffs, states[-1]),
            flops=work,
            moved=10 * rows_total * width,
            limit=n + n // 2,
            loose=1,
        )
        grad_rows, token = call(
            functools.partial(rows_kernel, n),
            [((SEG, width), BF), ((8, 128), F32)],
            scalars,
            (mine, other, upstream, middle, stats, tables),
            flops=LONG_FLOPS,
            moved=14 * SEG * width,
        )
        outs = call(
            ends_kernel,
            [((1, RANK, width), F32), ((1, RANK, width), F32), ((1, RANK), F32)],
            (),
            (slots, swap(slots), local, token),
            moved=20 * SEG * width,
            loose=1,
        )
        return (grad_rows, *outs)

    return on_device


def solution(mesh):
    return jax.shard_map(
        make_device_function(mesh.shape["dp"]),
        mesh=mesh,
        in_specs=(
            P(("groups", "dp"), None),
            P(("groups", "dp"), None),
            P(),
            P(None, ("dp", "tensor")),
            P(None, ("dp", "tensor")),
            P(("dp", "tensor"), None),
            P(("groups", "dp"), None, None),
            P(("groups", "dp"), None, None),
            P(("groups", "dp"), None),
            P("groups"),
            P("groups"),
            P("groups"),
        ),
        out_specs=(
            P(("groups", "dp"), None),
            P(("groups", "dp"), None, None),
            P(("groups", "dp"), None, None),
            P(("groups", "dp"), None),
        ),
        check_vma=False,
    )
```

```python
import functools

import jax
import jax.numpy as jnp
from jax import lax
from jax.experimental import pallas as pl
from jax.experimental.pallas import tpu as pltpu
from jax.sharding import PartitionSpec as P

SEG = 16
RANK = 8
PAD = 128
EPS = 1e-05
BF = jnp.bfloat16
F32 = jnp.float32


def dot_nn(a, b):
    return jnp.dot(a, b, preferred_element_type=F32)


def dot_nt(a, b):
    return lax.dot_general(a, b, (((1,), (1,)), ((), ())), preferred_element_type=F32)


def split(x):
    high = x.astype(BF)
    low = (x - high.astype(F32)).astype(BF)
    return high, low


def ring_order(n):
    if n == 8:
        return [0, 2, 4, 6, 7, 5, 3, 1]
    return list(range(n))


def place_of(n, d):
    if n == 8:
        return jnp.where(d % 2 == 0, d // 2, n - 1 - d // 2)
    return d


def device_at(n, p):
    if n == 8:
        return jnp.where(p < n // 2, 2 * p, 2 * (n - 1 - p) + 1)
    return p


def piece_devices(n, where_ref):
    half = n // 2 - 1
    steps = [0] + [-t for t in range(1, half + 1)] + [t for t in range(1, half + 1)] + [n // 2]
    me = place_of(n, where_ref[0])
    sign = 1 - 2 * where_ref[1]
    return [device_at(n, lax.rem(me + sign * step + n, n)) for step in steps]


def block_tenant(device, counts_ref, starts_ref, slots_ref):
    first = device * SEG
    begin, count, slot = starts_ref[0], counts_ref[0], slots_ref[0]
    for t in range(1, starts_ref.shape[0]):
        reached = starts_ref[t] <= first
        begin = jnp.where(reached, starts_ref[t], begin)
        count = jnp.where(reached, counts_ref[t], count)
        slot = jnp.where(reached, slots_ref[t], slot)
    return slot, count - (first - begin)


def tenant_mask(n, where_ref, counts_ref, starts_ref, slots_ref):
    shape = (n * SEG, n * SEG)
    row = lax.broadcasted_iota(jnp.int32, shape, 0)
    column = lax.broadcasted_iota(jnp.int32, shape, 1)
    devices = piece_devices(n, where_ref)
    row_slot = jnp.zeros(shape, jnp.int32)
    row_limit = jnp.zeros(shape, jnp.int32)
    column_slot = jnp.zeros(shape, jnp.int32)
    for k, device in enumerate(devices):
        slot, limit = block_tenant(device, counts_ref, starts_ref, slots_ref)
        here = row // SEG == k
        row_slot = jnp.where(here, slot, row_slot)
        row_limit = jnp.where(here, limit, row_limit)
        column_slot = jnp.where(column // SEG == k, device, column_slot)
    keep = (row_slot == column_slot) & (row % SEG < row_limit) & (column % SEG < RANK)
    return jnp.where(keep, 1.0, 0.0)


def columns_at(c, step):
    return pl.ds(pl.multiple_of(c * step, step), step)


def pack_upstream_kernel(
    upstream_hbm, basis_hbm, learned_hbm, bias_hbm, packed_ref, basis_ref, learned_ref, bias_ref, sems
):
    width = upstream_hbm.shape[1]
    copies = (
        pltpu.make_async_copy(upstream_hbm, packed_ref.at[:, :width], sems.at[0]),
        pltpu.make_async_copy(basis_hbm, basis_ref, sems.at[1]),
        pltpu.make_async_copy(learned_hbm, learned_ref, sems.at[2]),
        pltpu.make_async_copy(bias_hbm, bias_ref, sems.at[3]),
    )
    for copy in copies:
        copy.start()
    for copy in copies:
        copy.wait()
    half = width // 2
    table = jnp.concatenate(
        [basis_ref[0, :, half:].astype(F32), learned_ref[0, :, half:].astype(F32)], axis=0
    )
    packed_ref[:, width : width + half] = table.astype(BF)
    shape = (SEG, PAD)
    row = lax.broadcasted_iota(jnp.int32, shape, 0)
    lane = lax.broadcasted_iota(jnp.int32, shape, 1)
    bias = jnp.zeros(shape, F32)
    wide = bias_ref[...].astype(F32)
    for r in range(RANK):
        bias = jnp.where((row == RANK + r) & (lane == 0), wide[:, r : r + 1], bias)
    packed_ref[:, width + half :] = bias.astype(BF)


def pack_rows_kernel(hidden_hbm, basis_hbm, learned_hbm, packed_ref, basis_ref, learned_ref, sems):
    width = hidden_hbm.shape[1]
    copies = (
        pltpu.make_async_copy(hidden_hbm, packed_ref.at[:, :width], sems.at[0]),
        pltpu.make_async_copy(basis_hbm, basis_ref, sems.at[1]),
        pltpu.make_async_copy(learned_hbm, learned_ref, sems.at[2]),
    )
    for copy in copies:
        copy.start()
    for copy in copies:
        copy.wait()
    lane = lax.broadcasted_iota(jnp.int32, (SEG, PAD), 1)
    packed_ref[:, width : width + PAD] = jnp.where(lane == 0, 1.0, 0.0).astype(BF)
    half = width // 2
    table = jnp.concatenate(
        [basis_ref[0, :, :half].astype(F32), learned_ref[0, :, :half].astype(F32)], axis=0
    )
    packed_ref[:, width + PAD :] = table.astype(BF)


def mark_kernel(after, out_ref):
    del after
    out_ref[...] = jnp.zeros_like(out_ref)


def mask_kernel(n, where_ref, counts_ref, starts_ref, slots_ref, after, mask_ref):
    del after
    mask_ref[...] = tenant_mask(n, where_ref, counts_ref, starts_ref, slots_ref)


def back_kernel(n, *refs):
    pieces, (down_ref, upstream_ref, tables_ref, back_ref) = refs[:n], refs[-4:]
    width = upstream_ref.shape[1]
    for k, piece in enumerate(pieces):
        upstream_ref[k * SEG : (k + 1) * SEG, :] = piece[:, :width]
        tables_ref[k * SEG : (k + 1) * SEG, :] = piece[:, width:]
    back_ref[...] = dot_nt(upstream_ref[...], down_ref[...])


def hidden_kernel(n, step, *refs):
    pieces = refs[:n]
    (
        mask_ref,
        gain_ref,
        back_ref,
        right_ref,
        gate_ref,
        up_ref,
        own_ref,
        sent_ref,
        scaled_ref,
        rows_ref,
        tables_ref,
        middle_ref,
        coeffs_ref,
        pulled_ref,
        stats_ref,
        normed_ref,
        gate_t_ref,
        up_t_ref,
        gate_grad_ref,
        up_grad_ref,
    ) = refs[n:]
    row_total, width = middle_ref.shape
    chunks = width // step
    for k, piece in enumerate(pieces):
        rows_ref[k * SEG : (k + 1) * SEG, :] = piece[:, : width + PAD]
        tables_ref[k * SEG : (k + 1) * SEG, : width // 2] = piece[:, width + PAD :]
    tables_ref[:, width // 2 :] = right_ref[...]

    columns = tables_ref.shape[0]
    products = dot_nt(rows_ref[...], tables_ref[...])
    mask = mask_ref[...]
    coeffs = mask * (pltpu.roll(products, columns - RANK, 1) - products)
    coeffs_ref[...] = coeffs
    coeff_high, coeff_low = split(coeffs)

    column_zero = jnp.zeros((row_total, 1), F32)
    square_zero = jnp.zeros((row_total, columns), F32)
    squares, middle_tables = column_zero, square_zero
    for c in range(chunks):
        cols = slice(c * step, (c + 1) * step)
        table = tables_ref[:, cols]
        value = rows_ref[:, cols].astype(F32) + (
            dot_nn(coeff_high, table) + dot_nn(coeff_low, table)
        )
        value = value.astype(BF)
        middle_ref[:, cols] = value
        middle_tables = middle_tables + dot_nt(value, table)
        value = value.astype(F32)
        squares = squares + jnp.sum(value * value, axis=1, keepdims=True)
    inverse = lax.rsqrt(squares / width + EPS)

    for c in range(chunks):
        cols = slice(c * step, (c + 1) * step)
        value = middle_ref[:, cols].astype(F32) * inverse * gain_ref[:, cols]
        normed_ref[:, cols] = value.astype(BF)

    hidden = gate_ref.shape[1]
    tile = min(256, hidden)
    for j in range(hidden // tile):
        cols = slice(j * tile, (j + 1) * tile)
        gate = dot_nn(normed_ref[...], gate_ref[:, cols])
        gate_t_ref[cols, :] = gate_ref[:, cols].T
        upward = dot_nn(normed_ref[...], up_ref[:, cols])
        up_t_ref[cols, :] = up_ref[:, cols].T
        back = back_ref[:, cols]
        sigma = jax.nn.sigmoid(gate)
        gate_grad_ref[:, cols] = (back * upward * sigma * (1.0 + gate * (1.0 - sigma))).astype(BF)
        up_grad_ref[:, cols] = (back * gate * sigma).astype(BF)

    inner, scaled_tables = column_zero, square_zero
    for c in range(chunks):
        cols = slice(c * step, (c + 1) * step)
        value = dot_nn(gate_grad_ref[...], gate_t_ref[:, cols])
        value = value + dot_nn(up_grad_ref[...], up_t_ref[:, cols])
        value = value * gain_ref[:, cols]
        scaled_ref[:, cols] = value
        own_ref[:, cols] = value[:SEG]
        high = value.astype(BF)
        sent_ref[:, cols] = high[SEG:]
        scaled_tables = scaled_tables + dot_nt(high, tables_ref[:, cols])
        inner = inner + jnp.sum(value * middle_ref[:, cols].astype(F32), axis=1, keepdims=True)

    shrink = inverse * inverse * (inner / width)
    lane = lax.broadcasted_iota(jnp.int32, stats_ref.shape, 1)
    stats_ref[...] = jnp.where(lane == 0, inverse, shrink)
    pulled_ref[...] = mask * (inverse * (scaled_tables - shrink * middle_tables))


def slot_kernel(
    step,
    scaled_ref,
    rows_ref,
    middle_ref,
    coeffs_ref,
    pulled_ref,
    stats_ref,
    own_ref,
    sent_ref,
    weights_ref,
):
    row_total, width = middle_ref.shape
    inverse, shrink = stats_ref[:, 0:1], stats_ref[:, 1:2]
    pulled = pulled_ref[...]
    pulled = pltpu.roll(pulled, RANK, 1) - pulled
    weights_ref[:, :row_total] = coeffs_ref[...].T.astype(BF)
    weights_ref[:, row_total:] = pulled.T.astype(BF)

    for c in range(width // step):
        cols = slice(c * step, (c + 1) * step)
        value = inverse * (scaled_ref[:, cols] - middle_ref[:, cols].astype(F32) * shrink)
        both = jnp.concatenate([value.astype(BF), rows_ref[:, cols]], axis=0)
        value = dot_nn(weights_ref[...], both)
        sent_ref[:, cols] = value[SEG:].astype(BF)
        own_ref[:, cols] = value[:SEG]
    value = dot_nn(weights_ref[:, row_total:], rows_ref[:, width:])
    sent_ref[:, width:] = value[SEG:].astype(BF)
    own_ref[:, width:] = value[:SEG]


def local_kernel(step, mask_ref, rows_ref, tables_ref, upstream_ref, coeffs_ref, after, local_ref):
    del after
    row_total, width = upstream_ref.shape
    columns = tables_ref.shape[0]
    mask = mask_ref[...]
    lane = lax.broadcasted_iota(jnp.int32, (row_total, columns), 1)
    first = lane < RANK
    pulled = jnp.where(first, mask, 0.0) * dot_nt(upstream_ref[...], tables_ref[:, :width])
    pulled = pltpu.roll(pulled, RANK, 1) - pulled
    coeffs = jnp.where(first, coeffs_ref[...], 0.0)
    coeff_high, coeff_low = split(coeffs.T[:SEG])
    pulled_high, pulled_low = split(pulled.T[:SEG])

    def local_step(c, carry):
        cols = columns_at(c, step)
        upstream, rows = upstream_ref[:, cols], rows_ref[:, cols]
        value = dot_nn(coeff_high, upstream) + dot_nn(coeff_low, upstream)
        local_ref[:, cols] = value + (dot_nn(pulled_high, rows) + dot_nn(pulled_low, rows))
        return carry

    lax.fori_loop(0, width // step, local_step, 0)
    rows = rows_ref[:, width:]
    local_ref[:, width:] = dot_nn(pulled_high, rows) + dot_nn(pulled_low, rows)


def ends_kernel(mine_ref, other_ref, local_ref, after, basis_ref, learned_ref, bias_ref):
    del after
    width = basis_ref.shape[2]
    value = mine_ref[...] + other_ref[...] + local_ref[...]
    basis_ref[0, :, :] = value[:RANK, :width]
    learned_ref[0, :, :] = value[RANK:, :width]
    row = lax.broadcasted_iota(jnp.int32, (RANK, RANK), 0)
    lane = lax.broadcasted_iota(jnp.int32, (RANK, RANK), 1)
    bias = jnp.where(row == lane, value[RANK:, width : width + 1], 0.0)
    bias_ref[...] = jnp.sum(bias, axis=0, keepdims=True)


def rows_kernel(
    n,
    where_ref,
    counts_ref,
    starts_ref,
    slots_ref,
    mine_ref,
    other_ref,
    upstream_ref,
    middle_ref,
    stats_ref,
    tables_ref,
    out_ref,
    token_ref,
):
    width = out_ref.shape[1]
    token_ref[...] = jnp.zeros_like(token_ref)
    devices = piece_devices(n, where_ref)
    slot, limit = block_tenant(devices[0], counts_ref, starts_ref, slots_ref)
    which = 0
    for k, device in enumerate(devices):
        which = jnp.where(device == slot, k, which)
    table = tables_ref[pl.ds(pl.multiple_of(which * SEG, SEG), SEG), :width]
    middle = middle_ref[:SEG, :].astype(F32)
    inverse = stats_ref[:SEG, 0:1]
    scaled = mine_ref[...] + other_ref[...]
    inner = jnp.sum(scaled * middle, axis=1, keepdims=True) / width
    total = upstream_ref[:SEG, :].astype(F32) + inverse * (
        scaled - middle * (inverse * inverse * inner)
    )
    pulled = dot_nt(total.astype(BF), table)
    row = lax.broadcasted_iota(jnp.int32, (SEG, RANK), 0)
    pulled = jnp.where(row < limit, pulled[:, :RANK], 0.0)
    pulled = jnp.concatenate([-pulled, pulled], axis=1).astype(BF)
    out_ref[...] = (total + dot_nn(pulled, table)).astype(BF)


LOAD_FLOPS = 4 * 10**9
LONG_FLOPS = 40 * 10**9
SMEM_SPEC = pl.BlockSpec(memory_space=pltpu.SMEM)
VMEM_SPEC = pl.BlockSpec(memory_space=pltpu.VMEM)
ANY_SPEC = pl.BlockSpec(memory_space=pl.ANY)


def call(kernel, outs, scalars, arrays, scratch=(), flops=0, moved=0, limit=4, spec=None, loose=0):
    return pl.pallas_call(
        kernel,
        out_shape=tuple(jax.ShapeDtypeStruct(s, d) for s, d in outs),
        in_specs=[SMEM_SPEC] * len(scalars)
        + [spec or VMEM_SPEC] * (len(arrays) - loose)
        + [ANY_SPEC] * loose,
        out_specs=tuple(VMEM_SPEC for _ in outs),
        scratch_shapes=list(scratch),
        compiler_params=pltpu.CompilerParams(vmem_limit_bytes=limit * 1024 * 1024),
        cost_estimate=pl.CostEstimate(flops=flops, bytes_accessed=moved, transcendentals=0),
    )(*scalars, *arrays)


def resident(x):
    return pltpu.with_memory_space_constraint(x, pltpu.VMEM)


def remote(x):
    return pltpu.with_memory_space_constraint(x, pltpu.HBM)


def mark(after):
    (out,) = call(
        mark_kernel, [((8, 128), F32)], (), (after,), flops=LOAD_FLOPS, spec=pl.BlockSpec(memory_space=pl.ANY)
    )
    return out


def make_device_function(n):
    order = ring_order(n)
    place = {d: k for k, d in enumerate(order)}
    half = n // 2 - 1
    pairs = []
    for d in range(n):
        pairs.append((d * 2, order[(place[d] + 1) % n] * 2))
        pairs.append((d * 2 + 1, order[(place[d] - 1) % n] * 2 + 1))

    def hop(x):
        return lax.ppermute(x, ("dp", "tensor"), pairs)

    def swap(x):
        return lax.ppermute(x, "tensor", [(0, 1), (1, 0)])

    def gather(x):
        ahead, behind = [], []
        state = x
        for _ in range(half):
            state = hop(state)
            ahead.append(state)
            behind.append(swap(state))
        return [x] + ahead + behind + [hop(state)]

    def reduce(own, sent):
        other = swap(sent[: half * SEG])
        state = hop(sent[2 * half * SEG :])
        states = [state]
        for t in range(half - 1, -1, -1):
            mine = sent[(half + t) * SEG : (half + t + 1) * SEG].astype(F32)
            partner = other[t * SEG : (t + 1) * SEG].astype(F32)
            state = hop((state.astype(F32) + (mine + partner)).astype(BF))
            states.append(state)
        return own + state.astype(F32), states

    def on_device(
        hidden_in,
        grad_out,
        norm_gain,
        gate_weight,
        up_weight,
        down_weight,
        tenant_basis,
        tenant_learned,
        tenant_bias,
        row_counts,
        segment_starts,
        owner_slot,
    ):
        width = hidden_in.shape[1]
        hidden = gate_weight.shape[1]
        wide = width + PAD
        rows_total = n * SEG
        work = 2 * rows_total * width * hidden
        where = jnp.stack([lax.axis_index("dp"), lax.axis_index("tensor")]).astype(jnp.int32)
        scalars = (where, row_counts, segment_starts, owner_slot)
        tables_scratch = [
            pltpu.VMEM(tenant_basis.shape, BF),
            pltpu.VMEM(tenant_learned.shape, BF),
        ]
        hbm = pl.BlockSpec(memory_space=pltpu.MemorySpace.HBM)
        (packed_upstream,) = call(
            pack_upstream_kernel,
            [((SEG, width + width // 2 + PAD), BF)],
            (),
            tuple(remote(x) for x in (grad_out, tenant_basis, tenant_learned, tenant_bias)),
            scratch=tables_scratch
            + [pltpu.VMEM(tenant_bias.shape, BF), pltpu.SemaphoreType.DMA((4,))],
            moved=4 * SEG * wide * 2,
            spec=hbm,
        )
        (packed_rows,) = call(
            pack_rows_kernel,
            [((SEG, width + width // 2 + PAD), BF)],
            (),
            tuple(remote(x) for x in (hidden_in, tenant_basis, tenant_learned)),
            scratch=tables_scratch + [pltpu.SemaphoreType.DMA((3,))],
            moved=4 * SEG * wide * 2,
            spec=hbm,
        )
        upstream_pieces = gather(packed_upstream)
        row_pieces = gather(packed_rows)
        marks = tuple(mark(x) for x in (packed_rows, upstream_pieces[2]))
        (mask,) = call(
            functools.partial(mask_kernel, n),
            [((rows_total, rows_total), F32)],
            scalars,
            (upstream_pieces[1],),
            flops=LOAD_FLOPS,
            loose=1,
            limit=max(4, n // 2),
        )
        upstream, right, back = call(
            functools.partial(back_kernel, n),
            [
                ((rows_total, width), BF),
                ((rows_total, width // 2 + PAD), BF),
                ((rows_total, hidden), F32),
            ],
            (),
            (*upstream_pieces, *marks, resident(down_weight)),
            flops=LONG_FLOPS,
            moved=2 * width * hidden,
            limit=n,
        )
        own, sent, scaled, rows, tables, middle, coeffs, pulled, stats = call(
            functools.partial(hidden_kernel, n, 1024),
            [
                ((SEG, width), F32),
                ((rows_total - SEG, width), BF),
                ((rows_total, width), F32),
                ((rows_total, wide), BF),
                ((rows_total, wide), BF),
                ((rows_total, width), BF),
                ((rows_total, rows_total), F32),
                ((rows_total, rows_total), F32),
                ((rows_total, 128), F32),
            ],
            (),
            (
                *row_pieces,
                mask,
                norm_gain.reshape(1, width),
                back,
                right,
                resident(gate_weight),
                resident(up_weight),
            ),
            scratch=[
                pltpu.VMEM((rows_total, width), BF),
                pltpu.VMEM((hidden, width), BF),
                pltpu.VMEM((hidden, width), BF),
                pltpu.VMEM((rows_total, hidden), BF),
                pltpu.VMEM((rows_total, hidden), BF),
            ],
            flops=4 * work,
            moved=4 * width * hidden,
            limit=n + n // 2 + (4 * hidden * width) // 2**20,
        )
        own_slot, sent_slot = call(
            functools.partial(slot_kernel, 1024),
            [((SEG, wide), F32), ((rows_total - SEG, wide), BF)],
            (),
            (scaled, rows, middle, coeffs, pulled, stats),
            scratch=[pltpu.VMEM((rows_total, 2 * rows_total), BF)],
            flops=work,
            moved=10 * rows_total * width,
            limit=n + n // 2,
        )
        mine, states = reduce(own, sent)
        other = swap(mine)
        slots, _ = reduce(own_slot, sent_slot)
        (local,) = call(
            functools.partial(local_kernel, 1024),
            [((SEG, wide), F32)],
            (),
            (mask, rows, tables, upstream, coeffs, states[-1]),
            flops=work,
            moved=10 * rows_total * width,
            limit=n + n // 2,
            loose=1,
        )
        grad_rows, token = call(
            functools.partial(rows_kernel, n),
            [((SEG, width), BF), ((8, 128), F32)],
            scalars,
            (mine, other, upstream, middle, stats, tables),
            flops=LONG_FLOPS,
            moved=14 * SEG * width,
        )
        outs = call(
            ends_kernel,
            [((1, RANK, width), F32), ((1, RANK, width), F32), ((1, RANK), F32)],
            (),
            (slots, swap(slots), local, token),
            moved=20 * SEG * width,
            loose=1,
        )
        return (grad_rows, *outs)

    return on_device


def solution(mesh):
    return jax.shard_map(
        make_device_function(mesh.shape["dp"]),
        mesh=mesh,
        in_specs=(
            P(("groups", "dp"), None),
            P(("groups", "dp"), None),
            P(),
            P(None, ("dp", "tensor")),
            P(None, ("dp", "tensor")),
            P(("dp", "tensor"), None),
            P(("groups", "dp"), None, None),
            P(("groups", "dp"), None, None),
            P(("groups", "dp"), None),
            P("groups"),
            P("groups"),
            P("groups"),
        ),
        out_specs=(
            P(("groups", "dp"), None),
            P(("groups", "dp"), None, None),
            P(("groups", "dp"), None, None),
            P(("groups", "dp"), None),
        ),
        check_vma=False,
    )
```

```python
import functools

import jax
import jax.numpy as jnp
from jax import lax
from jax.experimental import pallas as pl
from jax.experimental.pallas import tpu as pltpu
from jax.sharding import PartitionSpec as P

SEG = 16
RANK = 8
PAD = 128
EPS = 1e-05
BF = jnp.bfloat16
F32 = jnp.float32


def dot_nn(a, b):
    return jnp.dot(a, b, preferred_element_type=F32)


def dot_nt(a, b):
    return lax.dot_general(a, b, (((1,), (1,)), ((), ())), preferred_element_type=F32)


def split(x):
    high = x.astype(BF)
    low = (x - high.astype(F32)).astype(BF)
    return high, low


def ring_order(n):
    if n == 8:
        return [0, 2, 4, 6, 7, 5, 3, 1]
    return list(range(n))


def place_of(n, d):
    if n == 8:
        return jnp.where(d % 2 == 0, d // 2, n - 1 - d // 2)
    return d


def device_at(n, p):
    if n == 8:
        return jnp.where(p < n // 2, 2 * p, 2 * (n - 1 - p) + 1)
    return p


def piece_devices(n, where_ref):
    half = n // 2 - 1
    steps = [0] + [-t for t in range(1, half + 1)] + [t for t in range(1, half + 1)] + [n // 2]
    me = place_of(n, where_ref[0])
    sign = 1 - 2 * where_ref[1]
    return [device_at(n, lax.rem(me + sign * step + n, n)) for step in steps]


def block_tenant(device, counts_ref, starts_ref, slots_ref):
    first = device * SEG
    begin, count, slot = starts_ref[0], counts_ref[0], slots_ref[0]
    for t in range(1, starts_ref.shape[0]):
        reached = starts_ref[t] <= first
        begin = jnp.where(reached, starts_ref[t], begin)
        count = jnp.where(reached, counts_ref[t], count)
        slot = jnp.where(reached, slots_ref[t], slot)
    return slot, count - (first - begin)


def tenant_mask(n, where_ref, counts_ref, starts_ref, slots_ref):
    shape = (n * SEG, n * SEG)
    row = lax.broadcasted_iota(jnp.int32, shape, 0)
    column = lax.broadcasted_iota(jnp.int32, shape, 1)
    devices = piece_devices(n, where_ref)
    row_slot = jnp.zeros(shape, jnp.int32)
    row_limit = jnp.zeros(shape, jnp.int32)
    column_slot = jnp.zeros(shape, jnp.int32)
    for k, device in enumerate(devices):
        slot, limit = block_tenant(device, counts_ref, starts_ref, slots_ref)
        here = row // SEG == k
        row_slot = jnp.where(here, slot, row_slot)
        row_limit = jnp.where(here, limit, row_limit)
        column_slot = jnp.where(column // SEG == k, device, column_slot)
    keep = (row_slot == column_slot) & (row % SEG < row_limit) & (column % SEG < RANK)
    return jnp.where(keep, 1.0, 0.0)


def columns_at(c, step):
    return pl.ds(pl.multiple_of(c * step, step), step)


def pack_upstream_kernel(
    upstream_hbm, basis_hbm, learned_hbm, bias_hbm, packed_ref, basis_ref, learned_ref, bias_ref, sems
):
    width = upstream_hbm.shape[1]
    copies = (
        pltpu.make_async_copy(upstream_hbm, packed_ref.at[:, :width], sems.at[0]),
        pltpu.make_async_copy(basis_hbm, basis_ref, sems.at[1]),
        pltpu.make_async_copy(learned_hbm, learned_ref, sems.at[2]),
        pltpu.make_async_copy(bias_hbm, bias_ref, sems.at[3]),
    )
    for copy in copies:
        copy.start()
    for copy in copies:
        copy.wait()
    half = width // 2
    table = jnp.concatenate(
        [basis_ref[0, :, half:].astype(F32), learned_ref[0, :, half:].astype(F32)], axis=0
    )
    packed_ref[:, width : width + half] = table.astype(BF)
    shape = (SEG, PAD)
    row = lax.broadcasted_iota(jnp.int32, shape, 0)
    lane = lax.broadcasted_iota(jnp.int32, shape, 1)
    bias = jnp.zeros(shape, F32)
    wide = bias_ref[...].astype(F32)
    for r in range(RANK):
        bias = jnp.where((row == RANK + r) & (lane == 0), wide[:, r : r + 1], bias)
    packed_ref[:, width + half :] = bias.astype(BF)


def pack_rows_kernel(hidden_hbm, basis_hbm, learned_hbm, packed_ref, basis_ref, learned_ref, sems):
    width = hidden_hbm.shape[1]
    copies = (
        pltpu.make_async_copy(hidden_hbm, packed_ref.at[:, :width], sems.at[0]),
        pltpu.make_async_copy(basis_hbm, basis_ref, sems.at[1]),
        pltpu.make_async_copy(learned_hbm, learned_ref, sems.at[2]),
    )
    for copy in copies:
        copy.start()
    for copy in copies:
        copy.wait()
    lane = lax.broadcasted_iota(jnp.int32, (SEG, PAD), 1)
    packed_ref[:, width : width + PAD] = jnp.where(lane == 0, 1.0, 0.0).astype(BF)
    half = width // 2
    table = jnp.concatenate(
        [basis_ref[0, :, :half].astype(F32), learned_ref[0, :, :half].astype(F32)], axis=0
    )
    packed_ref[:, width + PAD :] = table.astype(BF)


def mark_kernel(after, out_ref):
    del after
    out_ref[...] = jnp.zeros_like(out_ref)


def mask_kernel(n, where_ref, counts_ref, starts_ref, slots_ref, after, mask_ref):
    del after
    mask_ref[...] = tenant_mask(n, where_ref, counts_ref, starts_ref, slots_ref)


def back_kernel(n, *refs):
    pieces, (down_ref, upstream_ref, tables_ref, back_ref) = refs[:n], refs[-4:]
    width = upstream_ref.shape[1]
    for k, piece in enumerate(pieces):
        upstream_ref[k * SEG : (k + 1) * SEG, :] = piece[:, :width]
        tables_ref[k * SEG : (k + 1) * SEG, :] = piece[:, width:]
    back_ref[...] = dot_nt(upstream_ref[...], down_ref[...])


def hidden_kernel(n, step, *refs):
    pieces = refs[:n]
    (
        mask_ref,
        gain_ref,
        back_ref,
        right_ref,
        gate_ref,
        up_ref,
        own_ref,
        sent_ref,
        scaled_ref,
        rows_ref,
        tables_ref,
        middle_ref,
        coeffs_ref,
        pulled_ref,
        stats_ref,
        normed_ref,
        gate_t_ref,
        up_t_ref,
        gate_grad_ref,
        up_grad_ref,
    ) = refs[n:]
    row_total, width = middle_ref.shape
    chunks = width // step
    for k, piece in enumerate(pieces):
        rows_ref[k * SEG : (k + 1) * SEG, :] = piece[:, : width + PAD]
        tables_ref[k * SEG : (k + 1) * SEG, : width // 2] = piece[:, width + PAD :]
    tables_ref[:, width // 2 :] = right_ref[...]

    columns = tables_ref.shape[0]
    products = dot_nt(rows_ref[...], tables_ref[...])
    mask = mask_ref[...]
    coeffs = mask * (pltpu.roll(products, columns - RANK, 1) - products)
    coeffs_ref[...] = coeffs
    coeff_high, coeff_low = split(coeffs)

    column_zero = jnp.zeros((row_total, 1), F32)
    square_zero = jnp.zeros((row_total, columns), F32)
    squares, middle_tables = column_zero, square_zero
    for c in range(chunks):
        cols = slice(c * step, (c + 1) * step)
        table = tables_ref[:, cols]
        value = rows_ref[:, cols].astype(F32) + (
            dot_nn(coeff_high, table) + dot_nn(coeff_low, table)
        )
        value = value.astype(BF)
        middle_ref[:, cols] = value
        middle_tables = middle_tables + dot_nt(value, table)
        value = value.astype(F32)
        squares = squares + jnp.sum(value * value, axis=1, keepdims=True)
    inverse = lax.rsqrt(squares / width + EPS)

    for c in range(chunks):
        cols = slice(c * step, (c + 1) * step)
        value = middle_ref[:, cols].astype(F32) * inverse * gain_ref[:, cols]
        normed_ref[:, cols] = value.astype(BF)

    hidden = gate_ref.shape[1]
    tile = min(256, hidden)
    for j in range(hidden // tile):
        cols = slice(j * tile, (j + 1) * tile)
        gate = dot_nn(normed_ref[...], gate_ref[:, cols])
        gate_t_ref[cols, :] = gate_ref[:, cols].T
        upward = dot_nn(normed_ref[...], up_ref[:, cols])
        up_t_ref[cols, :] = up_ref[:, cols].T
        back = back_ref[:, cols]
        sigma = jax.nn.sigmoid(gate)
        gate_grad_ref[:, cols] = (back * upward * sigma * (1.0 + gate * (1.0 - sigma))).astype(BF)
        up_grad_ref[:, cols] = (back * gate * sigma).astype(BF)

    inner, scaled_tables = column_zero, square_zero
    for c in range(chunks):
        cols = slice(c * step, (c + 1) * step)
        value = dot_nn(gate_grad_ref[...], gate_t_ref[:, cols])
        value = value + dot_nn(up_grad_ref[...], up_t_ref[:, cols])
        value = value * gain_ref[:, cols]
        scaled_ref[:, cols] = value
        own_ref[:, cols] = value[:SEG]
        high = value.astype(BF)
        sent_ref[:, cols] = high[SEG:]
        scaled_tables = scaled_tables + dot_nt(high, tables_ref[:, cols])
        inner = inner + jnp.sum(value * middle_ref[:, cols].astype(F32), axis=1, keepdims=True)

    shrink = inverse * inverse * (inner / width)
    lane = lax.broadcasted_iota(jnp.int32, stats_ref.shape, 1)
    stats_ref[...] = jnp.where(lane == 0, inverse, shrink)
    pulled_ref[...] = mask * (inverse * (scaled_tables - shrink * middle_tables))


def slot_kernel(
    step,
    scaled_ref,
    rows_ref,
    middle_ref,
    coeffs_ref,
    pulled_ref,
    stats_ref,
    own_ref,
    sent_ref,
    weights_ref,
):
    row_total, width = middle_ref.shape
    inverse, shrink = stats_ref[:, 0:1], stats_ref[:, 1:2]
    pulled = pulled_ref[...]
    pulled = pltpu.roll(pulled, RANK, 1) - pulled
    weights_ref[:, :row_total] = coeffs_ref[...].T.astype(BF)
    weights_ref[:, row_total:] = pulled.T.astype(BF)

    for c in range(width // step):
        cols = slice(c * step, (c + 1) * step)
        value = inverse * (scaled_ref[:, cols] - middle_ref[:, cols].astype(F32) * shrink)
        both = jnp.concatenate([value.astype(BF), rows_ref[:, cols]], axis=0)
        value = dot_nn(weights_ref[...], both)
        sent_ref[:, cols] = value[SEG:].astype(BF)
        own_ref[:, cols] = value[:SEG]
    value = dot_nn(weights_ref[:, row_total:], rows_ref[:, width:])
    sent_ref[:, width:] = value[SEG:].astype(BF)
    own_ref[:, width:] = value[:SEG]


def local_kernel(step, mask_ref, rows_ref, tables_ref, upstream_ref, coeffs_ref, after, local_ref):
    del after
    row_total, width = upstream_ref.shape
    columns = tables_ref.shape[0]
    mask = mask_ref[...]
    lane = lax.broadcasted_iota(jnp.int32, (row_total, columns), 1)
    first = lane < RANK
    pulled = jnp.where(first, mask, 0.0) * dot_nt(upstream_ref[...], tables_ref[:, :width])
    pulled = pltpu.roll(pulled, RANK, 1) - pulled
    coeffs = jnp.where(first, coeffs_ref[...], 0.0)
    coeff_high, coeff_low = split(coeffs.T[:SEG])
    pulled_high, pulled_low = split(pulled.T[:SEG])

    def local_step(c, carry):
        cols = columns_at(c, step)
        upstream, rows = upstream_ref[:, cols], rows_ref[:, cols]
        value = dot_nn(coeff_high, upstream) + dot_nn(coeff_low, upstream)
        local_ref[:, cols] = value + (dot_nn(pulled_high, rows) + dot_nn(pulled_low, rows))
        return carry

    lax.fori_loop(0, width // step, local_step, 0)
    rows = rows_ref[:, width:]
    local_ref[:, width:] = dot_nn(pulled_high, rows) + dot_nn(pulled_low, rows)


def ends_kernel(mine_ref, other_ref, local_ref, after, basis_ref, learned_ref, bias_ref):
    del after
    width = basis_ref.shape[2]
    value = mine_ref[...] + other_ref[...] + local_ref[...]
    basis_ref[0, :, :] = value[:RANK, :width]
    learned_ref[0, :, :] = value[RANK:, :width]
    row = lax.broadcasted_iota(jnp.int32, (RANK, RANK), 0)
    lane = lax.broadcasted_iota(jnp.int32, (RANK, RANK), 1)
    bias = jnp.where(row == lane, value[RANK:, width : width + 1], 0.0)
    bias_ref[...] = jnp.sum(bias, axis=0, keepdims=True)


def rows_kernel(
    n,
    where_ref,
    counts_ref,
    starts_ref,
    slots_ref,
    mine_ref,
    other_ref,
    upstream_ref,
    middle_ref,
    stats_ref,
    tables_ref,
    out_ref,
    token_ref,
):
    width = out_ref.shape[1]
    token_ref[...] = jnp.zeros_like(token_ref)
    devices = piece_devices(n, where_ref)
    slot, limit = block_tenant(devices[0], counts_ref, starts_ref, slots_ref)
    which = 0
    for k, device in enumerate(devices):
        which = jnp.where(device == slot, k, which)
    table = tables_ref[pl.ds(pl.multiple_of(which * SEG, SEG), SEG), :width]
    middle = middle_ref[:SEG, :].astype(F32)
    inverse = stats_ref[:SEG, 0:1]
    scaled = mine_ref[...] + other_ref[...]
    inner = jnp.sum(scaled * middle, axis=1, keepdims=True) / width
    total = upstream_ref[:SEG, :].astype(F32) + inverse * (
        scaled - middle * (inverse * inverse * inner)
    )
    pulled = dot_nt(total.astype(BF), table)
    row = lax.broadcasted_iota(jnp.int32, (SEG, RANK), 0)
    pulled = jnp.where(row < limit, pulled[:, :RANK], 0.0)
    pulled = jnp.concatenate([-pulled, pulled], axis=1).astype(BF)
    out_ref[...] = (total + dot_nn(pulled, table)).astype(BF)


LOAD_FLOPS = 4 * 10**9
LONG_FLOPS = 40 * 10**9
SMEM_SPEC = pl.BlockSpec(memory_space=pltpu.SMEM)
VMEM_SPEC = pl.BlockSpec(memory_space=pltpu.VMEM)
ANY_SPEC = pl.BlockSpec(memory_space=pl.ANY)


def call(kernel, outs, scalars, arrays, scratch=(), flops=0, moved=0, limit=4, spec=None, loose=0):
    return pl.pallas_call(
        kernel,
        out_shape=tuple(jax.ShapeDtypeStruct(s, d) for s, d in outs),
        in_specs=[SMEM_SPEC] * len(scalars)
        + [spec or VMEM_SPEC] * (len(arrays) - loose)
        + [ANY_SPEC] * loose,
        out_specs=tuple(VMEM_SPEC for _ in outs),
        scratch_shapes=list(scratch),
        compiler_params=pltpu.CompilerParams(vmem_limit_bytes=limit * 1024 * 1024),
        cost_estimate=pl.CostEstimate(flops=flops, bytes_accessed=moved, transcendentals=0),
    )(*scalars, *arrays)


def resident(x):
    return pltpu.with_memory_space_constraint(x, pltpu.VMEM)


def remote(x):
    return pltpu.with_memory_space_constraint(x, pltpu.HBM)


def mark(after):
    (out,) = call(
        mark_kernel, [((8, 128), F32)], (), (after,), flops=LOAD_FLOPS, spec=pl.BlockSpec(memory_space=pl.ANY)
    )
    return out


def make_device_function(n):
    order = ring_order(n)
    place = {d: k for k, d in enumerate(order)}
    half = n // 2 - 1
    pairs = []
    for d in range(n):
        pairs.append((d * 2, order[(place[d] + 1) % n] * 2))
        pairs.append((d * 2 + 1, order[(place[d] - 1) % n] * 2 + 1))

    def hop(x):
        return lax.ppermute(x, ("dp", "tensor"), pairs)

    def swap(x):
        return lax.ppermute(x, "tensor", [(0, 1), (1, 0)])

    def gather(x):
        ahead, behind = [], []
        state = x
        for _ in range(half):
            state = hop(state)
            ahead.append(state)
            behind.append(swap(state))
        return [x] + ahead + behind + [hop(state)]

    def reduce(own, sent):
        other = swap(sent[: half * SEG])
        state = hop(sent[2 * half * SEG :])
        states = [state]
        for t in range(half - 1, -1, -1):
            mine = sent[(half + t) * SEG : (half + t + 1) * SEG].astype(F32)
            partner = other[t * SEG : (t + 1) * SEG].astype(F32)
            state = hop((state.astype(F32) + (mine + partner)).astype(BF))
            states.append(state)
        return own + state.astype(F32), states

    def on_device(
        hidden_in,
        grad_out,
        norm_gain,
        gate_weight,
        up_weight,
        down_weight,
        tenant_basis,
        tenant_learned,
        tenant_bias,
        row_counts,
        segment_starts,
        owner_slot,
    ):
        width = hidden_in.shape[1]
        hidden = gate_weight.shape[1]
        wide = width + PAD
        rows_total = n * SEG
        work = 2 * rows_total * width * hidden
        where = jnp.stack([lax.axis_index("dp"), lax.axis_index("tensor")]).astype(jnp.int32)
        scalars = (where, row_counts, segment_starts, owner_slot)
        tables_scratch = [
            pltpu.VMEM(tenant_basis.shape, BF),
            pltpu.VMEM(tenant_learned.shape, BF),
        ]
        hbm = pl.BlockSpec(memory_space=pltpu.MemorySpace.HBM)
        (packed_upstream,) = call(
            pack_upstream_kernel,
            [((SEG, width + width // 2 + PAD), BF)],
            (),
            tuple(remote(x) for x in (grad_out, tenant_basis, tenant_learned, tenant_bias)),
            scratch=tables_scratch
            + [pltpu.VMEM(tenant_bias.shape, BF), pltpu.SemaphoreType.DMA((4,))],
            moved=4 * SEG * wide * 2,
            spec=hbm,
        )
        (packed_rows,) = call(
            pack_rows_kernel,
            [((SEG, width + width // 2 + PAD), BF)],
            (),
            tuple(remote(x) for x in (hidden_in, tenant_basis, tenant_learned)),
            scratch=tables_scratch + [pltpu.SemaphoreType.DMA((3,))],
            moved=4 * SEG * wide * 2,
            spec=hbm,
        )
        upstream_pieces = gather(packed_upstream)
        row_pieces = gather(packed_rows)
        marks = tuple(mark(x) for x in (packed_rows, upstream_pieces[2]))
        (mask,) = call(
            functools.partial(mask_kernel, n),
            [((rows_total, rows_total), F32)],
            scalars,
            (upstream_pieces[1],),
            flops=LOAD_FLOPS,
            loose=1,
            limit=max(4, n // 2),
        )
        upstream, right, back = call(
            functools.partial(back_kernel, n),
            [
                ((rows_total, width), BF),
                ((rows_total, width // 2 + PAD), BF),
                ((rows_total, hidden), F32),
            ],
            (),
            (*upstream_pieces, *marks, resident(down_weight)),
            flops=LONG_FLOPS,
            moved=2 * width * hidden,
            limit=n,
        )
        own, sent, scaled, rows, tables, middle, coeffs, pulled, stats = call(
            functools.partial(hidden_kernel, n, 2048),
            [
                ((SEG, width), F32),
                ((rows_total - SEG, width), BF),
                ((rows_total, width), F32),
                ((rows_total, wide), BF),
                ((rows_total, wide), BF),
                ((rows_total, width), BF),
                ((rows_total, rows_total), F32),
                ((rows_total, rows_total), F32),
                ((rows_total, 128), F32),
            ],
            (),
            (
                *row_pieces,
                mask,
                norm_gain.reshape(1, width),
                back,
                right,
                resident(gate_weight),
                resident(up_weight),
            ),
            scratch=[
                pltpu.VMEM((rows_total, width), BF),
                pltpu.VMEM((hidden, width), BF),
                pltpu.VMEM((hidden, width), BF),
                pltpu.VMEM((rows_total, hidden), BF),
                pltpu.VMEM((rows_total, hidden), BF),
            ],
            flops=4 * work,
            moved=4 * width * hidden,
            limit=n + n // 2 + (4 * hidden * width) // 2**20,
        )
        own_slot, sent_slot = call(
            functools.partial(slot_kernel, 1024),
            [((SEG, wide), F32), ((rows_total - SEG, wide), BF)],
            (),
            (scaled, rows, middle, coeffs, pulled, stats),
            scratch=[pltpu.VMEM((rows_total, 2 * rows_total), BF)],
            flops=work,
            moved=10 * rows_total * width,
            limit=n + n // 2,
        )
        mine, states = reduce(own, sent)
        other = swap(mine)
        slots, _ = reduce(own_slot, sent_slot)
        (local,) = call(
            functools.partial(local_kernel, 1024),
            [((SEG, wide), F32)],
            (),
            (mask, rows, tables, upstream, coeffs, states[-1]),
            flops=work,
            moved=10 * rows_total * width,
            limit=n + n // 2,
            loose=1,
        )
        grad_rows, token = call(
            functools.partial(rows_kernel, n),
            [((SEG, width), BF), ((8, 128), F32)],
            scalars,
            (mine, other, upstream, middle, stats, tables),
            flops=LONG_FLOPS,
            moved=14 * SEG * width,
        )
        outs = call(
            ends_kernel,
            [((1, RANK, width), F32), ((1, RANK, width), F32), ((1, RANK), F32)],
            (),
            (slots, swap(slots), local, token),
            moved=20 * SEG * width,
            loose=1,
        )
        return (grad_rows, *outs)

    return on_device


def solution(mesh):
    return jax.shard_map(
        make_device_function(mesh.shape["dp"]),
        mesh=mesh,
        in_specs=(
            P(("groups", "dp"), None),
            P(("groups", "dp"), None),
            P(),
            P(None, ("dp", "tensor")),
            P(None, ("dp", "tensor")),
            P(("dp", "tensor"), None),
            P(("groups", "dp"), None, None),
            P(("groups", "dp"), None, None),
            P(("groups", "dp"), None),
            P("groups"),
            P("groups"),
            P("groups"),
        ),
        out_specs=(
            P(("groups", "dp"), None),
            P(("groups", "dp"), None, None),
            P(("groups", "dp"), None, None),
            P(("groups", "dp"), None),
        ),
        check_vma=False,
    )
```
